128 devices in a mesh: gx: 16 (over y, x_lo, core), gy: 8 (over x_hi, z).
Axes of the slice: x: 4 (x_hi: 2, x_lo: 2; x = x_hi * 2 + x_lo), y: 4, z: 4, core: 2. Of those that a mesh axis runs over, the one named last changes fastest.
Arguments:
- temp_start: float32 [8, 4096, 4096], P(None, ('gx', 'gy')), may hold values from -6 to 6
- heat_input: float32 [8, 4096, 4096], P(None, ('gx', 'gy')), may hold values from -3 to 3
- lateral: float32 [8], replicated, may hold values from 0.03 to 0.15
- vertical: float32 [7], replicated, may hold values from 0.03 to 0.15
- weighting: float32 [8], replicated, may hold values from -1 to 1
- modulus: float32 [4096, 4096], P('gx', 'gy'), may hold values from 0.3 to 3
- warp_prev: float32 [4096, 4096], P('gx', 'gy'), may hold values from -6 to 6
- joint_cell: int32 [262144], P(('gx', 'gy')), may hold values from 0 to 131071
- joint_owner: int32 [262144, 1], P(('gx', 'gy')), may hold values from 0 to 127; in each aligned block of 2048 rows (0 to 2047, 2048 to 4095, ...) at most 48 rows name the same one
- joint_strain: float32 [2, 128, 6144], P(None, ('gx', 'gy')), may hold values from -4 to 4
- joint_resist: float32 [128, 6144], P(('gx', 'gy')), may hold values from 1 to 2
Outputs:
- warpage: float32 [4096, 4096], P('gx', 'gy')
- strain_next: float32 [2, 128, 6144], P(None, ('gx', 'gy'))
- resist_next: float32 [128, 6144], P(('gx', 'gy'))
The draws below stay inside these ranges and needn't reach their ends.
Inputs may be any that keep to these rules, and one draw needn't show every extreme that they name: `joint_owner`: among the 2048 joints of one device at most 48 have the same owner, and on some device exactly 48 do.
All inputs are finite; a program needn't handle non-finite values.
Results may differ from the reference program's by a relative error of at most 0.0003.
Values sent between devices are 32-bit elements; how exact they have to be, the bound alone decides.
A program may use at most 320 MiB of HBM per device.

```python
import math
import jax
import jax.numpy as jnp
import numpy as np
from jax import lax

CM = 512
LAYERS = 8
STEPS = 2
SWEEPS = 3
JPD = 2048
RM = 256
NR = 4096
C = 4096
JOINTS = 262144
CAP = 48
N_GX = 16
N_GY = 8


def place_ends(values, own_key, low, high):
    shape = values.shape
    place = [jax.random.randint(jax.random.fold_in(own_key, axis), (), 0, shape[axis]) for axis in range(len(shape))]
    values = values.at[tuple(place)].set(low)
    longest = shape.index(max(shape))
    place[longest] = (place[longest] + 1) % shape[longest]
    return values.at[tuple(place)].set(high)


def levels(key, dims, pieces, smallest, largest):
    level, own = 1.0, jax.random.fold_in(key, 6)
    for axis_at, parts in pieces:
        heights = jnp.exp(jax.random.uniform(jax.random.fold_in(own, axis_at), (parts,), jnp.float32, smallest / len(pieces), largest / len(pieces)))
        level = level * jnp.repeat(heights, dims[axis_at] // parts).reshape([-1 if axis == axis_at else 1 for axis in range(len(dims))])
    return level


def deal_out(key, own, number, rows, amount, top, most, lean):
    order = jax.random.permutation(key, amount)
    crowded, ordinary = portions_of(amount, rows * top, most, lean, True), portions_of(amount, rows * top, most, lean, False)
    places = jnp.arange(amount)

    def named(lengths, offset_by):
        used = int((lengths > 0).sum())
        fixed = max(1, used // 4)
        shifted = fixed + (places - fixed + offset_by * (used - fixed)) % max(1, amount - fixed)
        return jnp.zeros((amount,), jnp.int32).at[order[jnp.where(places < fixed, places, shifted)]].set(jnp.asarray(lengths, jnp.int32))

    lengths = jnp.where(number % 4 == 0, named(crowded, number // 4), named(ordinary, number - number // 4 - 1))
    mixed = jax.random.permutation(jax.random.fold_in(own, 3), amount)
    giver, taker = mixed[0:amount // 2 * 2:2], mixed[1:amount // 2 * 2:2]
    slack = jnp.minimum(lengths[giver] - 1, most - lengths[taker]) // 2
    slack = jnp.where((giver == order[0]) | (taker == order[0]) | (lengths[taker] == 0), 0, jnp.maximum(slack, 0))
    shifted = jax.random.randint(jax.random.fold_in(own, 4), (amount // 2,), 0, 1 << 20) % (slack + 1)
    lengths = lengths.at[giver].add(-shifted).at[taker].add(shifted)
    labels = jnp.searchsorted(jnp.cumsum(lengths), jnp.arange(rows * top), side="right").astype(jnp.int32)
    table = labels.reshape(top, rows).T
    table = table[jax.random.permutation(jax.random.fold_in(own, 1), rows)]
    offset_by = jax.random.randint(jax.random.fold_in(own, 2), (rows, 1), 0, top)
    return jnp.take_along_axis(table, (jnp.arange(top)[None, :] + offset_by) % top, axis=1)


def portions_of(number_of, total, most, lean, full):
    portions = [(1 << 20) // math.isqrt(rank ** lean) + 1 for rank in range(1, number_of + 1)]
    largest = most if full else min(most, max(-(-total // number_of), total * portions[0] // sum(portions)))
    least = 1 if total - largest >= number_of - 1 else 0
    given, surplus = [largest] + [least] * (number_of - 1), total - largest - least * (number_of - 1)
    while surplus > 0:
        free = [i for i in range(1, number_of) if given[i] < largest] or [i for i in range(1, number_of) if given[i] < most]
        pool, remaining = sum([portions[i] for i in free]), surplus
        for i in free:
            addition = min(most - given[i], max(1, remaining * portions[i] // pool), surplus)
            given[i] = given[i] + addition
            surplus = surplus - addition
    return np.array(given)


def gaussian(own_key, shape, scale, bound, split=(), held_as=jnp.bfloat16):
    entries = scale * jax.random.normal(own_key, shape, jnp.float32)
    if split:
        entries = entries * levels(own_key, shape, split, -0.22, 0.18)
    return jnp.clip(entries, -bound, bound).astype(held_as)


def setup_inputs(seed: int = 0) -> dict:
    streams_of = jax.random.split(jax.random.key(seed), 12)
    temp_start = gaussian(streams_of[0], (LAYERS, NR, C), 1.0, 6.0, ((1, 128),), jnp.float32)
    heat_input = gaussian(streams_of[1], (LAYERS, NR, C), 0.2, 3.0, ((1, 128),), jnp.float32)
    lateral = jnp.clip(jnp.exp(jax.random.uniform(streams_of[2], (LAYERS,), jnp.float32, math.log(0.03), math.log(0.15))), 0.03, 0.15)
    vertical = jnp.clip(jnp.exp(jax.random.uniform(streams_of[3], (LAYERS - 1,), jnp.float32, math.log(0.03), math.log(0.15))), 0.03, 0.15)
    weighting = jnp.clip(jax.random.uniform(streams_of[4], (LAYERS,), jnp.float32, -1.0, 1.0), -1.0, 1.0)
    modulus = jnp.clip(jnp.exp(math.log(3.0) - 2.3025851 * jax.random.uniform(streams_of[5], (NR, C), jnp.float32) ** levels(streams_of[5], (NR, C), ((0, 16), (1, 8)), -0.2, 0.2)), 0.3, 3.0)
    warp_prev = gaussian(streams_of[6], (NR, C), 0.5, 6.0, ((0, 16), (1, 8)), jnp.float32)
    joint_cell = place_ends(jax.random.randint(streams_of[7], (JOINTS,), 0, RM * CM), jax.random.fold_in(streams_of[7], 1), 0, (RM * CM) - 1).astype(jnp.int32)
    joint_owner_keys = jax.random.split(jax.random.fold_in(streams_of[8], 1), JOINTS // JPD)
    joint_owner_turns = jax.random.permutation(jax.random.fold_in(streams_of[8], 3), JOINTS // JPD)
    joint_owner = jax.vmap(lambda own, number: deal_out(jax.random.fold_in(streams_of[8], 2), own, number, JPD, N_GX * N_GY, 1, CAP, 2))(joint_owner_keys, joint_owner_turns).reshape((JOINTS, 1))
    joint_strain = gaussian(streams_of[9], (2, N_GX * N_GY, N_GX * N_GY * CAP), 0.3, 4.0, ((1, 128),), jnp.float32)
    joint_resist = jnp.clip(1.0 + 1.0 * jax.random.uniform(streams_of[10], (N_GX * N_GY, N_GX * N_GY * CAP), jnp.float32) ** levels(streams_of[10], (N_GX * N_GY, N_GX * N_GY * CAP), ((0, 128),), -0.2, 0.2), 1.0, 2.0)
    return dict(temp_start=temp_start, heat_input=heat_input, lateral=lateral, vertical=vertical, weighting=weighting, modulus=modulus, warp_prev=warp_prev, joint_cell=joint_cell, joint_owner=joint_owner, joint_strain=joint_strain, joint_resist=joint_resist)


stiffness = 0.2
shear_mod = 0.6
rate_scale = 0.5
sat_level = 2.5
sat_power = 0.3
harden = 2.0


def thermal_step(ext, heat_rows, lateral, vertical):
    cols = jnp.pad(ext, ((0, 0), (0, 0), (1, 1)))
    center = ext[:, 1:-1]
    lap = ext[:, 2:] + ext[:, :-2] + cols[:, 1:-1, 2:] + cols[:, 1:-1, :-2] - 4.0 * center
    flux = vertical[:, None, None] * (center[1:] - center[:-1])
    vert = jnp.pad(flux, ((0, 1), (0, 0), (0, 0))) - jnp.pad(flux, ((1, 0), (0, 0), (0, 0)))
    return center + lateral[:, None, None] * lap + vert + heat_rows


def moment_of(field, weighting):
    total = weighting[0] * field[0]
    for layer in range(1, field.shape[0]):
        total = total + weighting[layer] * field[layer]
    return total


def sweep(w_pad, e_pad, load):
    center = e_pad[1:-1, 1:-1]
    e_up = 0.5 * (center + e_pad[:-2, 1:-1])
    e_down = 0.5 * (center + e_pad[2:, 1:-1])
    e_left = 0.5 * (center + e_pad[1:-1, :-2])
    e_right = 0.5 * (center + e_pad[1:-1, 2:])
    numer = load + e_up * w_pad[:-2, 1:-1] + e_down * w_pad[2:, 1:-1] + e_left * w_pad[1:-1, :-2] + e_right * w_pad[1:-1, 2:]
    denom = stiffness + e_up + e_down + e_left + e_right
    return numer / denom


def pack_joints(cells, owners, warp_flat, prev_flat, top_flat, devices, cap):
    increment = warp_flat[cells] - prev_flat[cells]
    theta = top_flat[cells]
    values = jnp.stack([increment, theta, jnp.ones_like(theta)])
    onehot = (owners[:, None] == jnp.arange(devices, dtype=jnp.int32)[None, :]).astype(jnp.int32)
    ranks = jnp.sum(jnp.cumsum(onehot, axis=0) * onehot, axis=1) - 1
    slots = (owners * cap + ranks).astype(jnp.int32)
    return jnp.zeros((3, devices * cap), jnp.float32).at[:, slots].set(values)


def anand(strain, resist, recv):
    total, inelastic = strain[0], strain[1]
    increment, theta, live = recv[0], recv[1], recv[2]
    total_new = total + increment
    arrhen = jnp.exp(2.0 - 2.0 / (1.0 + 0.1 * theta * theta))
    hyper = jnp.sinh(shear_mod * (total_new - inelastic) / resist)
    rate = rate_scale * arrhen * hyper * jnp.abs(hyper)
    inelastic_new = inelastic + rate
    target = sat_level * jnp.power(1.0 + jnp.abs(rate) / arrhen, sat_power)
    resist_new = resist + harden * (1.0 - resist / target) * jnp.abs(rate)
    keep = live > 0.5
    strain_out = jnp.stack([jnp.where(keep, total_new, total), jnp.where(keep, inelastic_new, inelastic)])
    return strain_out, jnp.where(keep, resist_new, resist)


def as_tiles(field):
    return field.reshape(N_GX, RM, N_GY, CM).transpose(0, 2, 1, 3).reshape(N_GX * N_GY, RM * CM)


def reference(temp_start, heat_input, lateral, vertical, weighting, modulus, warp_prev, joint_cell, joint_owner, joint_strain, joint_resist):
    temp = temp_start
    for step in range(STEPS):
        ext = jnp.pad(temp, ((0, 0), (1, 1), (0, 0)))
        temp = thermal_step(ext, heat_input, lateral, vertical)
    load = moment_of(temp, weighting)
    top = temp[-1]
    e_pad = jnp.pad(modulus, 1)
    warp = warp_prev
    for step in range(SWEEPS):
        warp = sweep(jnp.pad(warp, 1), e_pad, load)
    devices = N_GX * N_GY
    warp_tiles = as_tiles(warp)
    prev_tiles = as_tiles(warp_prev)
    top_tiles = as_tiles(top)
    cells = joint_cell.reshape(devices, JPD)
    owners = joint_owner.reshape(devices, JPD)

    def one_source(args):
        return pack_joints(args[0], args[1], args[2], args[3], args[4], devices, CAP)

    sent = lax.map(one_source, (cells, owners, warp_tiles, prev_tiles, top_tiles))
    recv = sent.reshape(devices, 3, devices, CAP).transpose(1, 2, 0, 3).reshape(3, devices, devices * CAP)
    strain_next, resist_next = anand(joint_strain, joint_resist, recv)
    return warp, strain_next, resist_next
```

```python
import functools

import jax
import jax.numpy as jnp
from jax import lax
from jax.experimental import pallas as pl
from jax.experimental.pallas import tpu as pltpu
from jax.sharding import PartitionSpec as P

MESH = pl.DeviceIdType.MESH
F32 = jnp.float32
BF16 = jnp.bfloat16

stiffness = 0.2
shear_mod = 0.6
rate_scale = 0.5
sat_level = 2.5
sat_power = 0.3
harden = 2.0
LN2 = 0.6931471805599453


def iota(shape, dim):
    return lax.broadcasted_iota(jnp.int32, shape, dim)


def split(x):
    hi = x.astype(BF16)
    return hi, (x - hi.astype(F32)).astype(BF16)


def layer_weights(lat, ver, w):
    n = len(w)

    def add(x, y):
        return y if x is None else x if y is None else x + y

    def mul(x, y):
        return None if x is None else x * y

    def vert(x):
        out = []
        for l in range(n):
            keep = 1.0
            if l < n - 1:
                keep = keep - ver[l]
            if l > 0:
                keep = keep - ver[l - 1]
            total = mul(x[l], keep)
            if l > 0:
                total = add(total, mul(x[l - 1], ver[l - 1]))
            if l < n - 1:
                total = add(total, mul(x[l + 1], ver[l]))
            out.append(total)
        return out

    u = vert(w)
    wd = [mul(x, d) for x, d in zip(w, lat)]
    a0 = vert(u)
    a1 = [add(mul(x, d), y) for x, d, y in zip(u, lat, vert(wd))]
    a2 = [mul(x, d) for x, d in zip(wd, lat)]
    b0 = [add(x, y) for x, y in zip(u, w)]
    return (a0, b0), (a1, wd), (a2, [None] * n)


def kernel(
    n_gx,
    n_gy,
    temp_ref,
    heat_ref,
    lat_ref,
    ver_ref,
    wei_ref,
    mod_ref,
    prev_ref,
    cell_ref,
    owner_ref,
    strain_ref,
    resist_ref,
    warp_out,
    strain_out,
    resist_out,
    tbuf,
    hbuf,
    sums,
    msg_s,
    msg_r,
    cross_s,
    cross_r,
    col_s,
    col_r,
    row_s,
    row_r,
    mw,
    wbuf,
    coef,
    load,
    edges,
    top,
    oh_row,
    oh_own,
    slot_of,
    ft_hi,
    ft_lo,
    inc_of,
    theta_of,
    out1_s,
    out1_r,
    out2_s,
    out2_r,
    load_sem,
    aux_sem,
    out_sem,
    col_ss,
    col_rs,
    row_ss,
    row_rs,
    msg_ss,
    msg_rs,
    cross_ss,
    cross_rs,
    one_ss,
    one_rs,
    two_ss,
    two_rs,
):
    layers, tr, columns = temp_ref.shape
    rm, cm = mod_ref.shape
    blocks = tr // 8
    nrow = rm + 8
    ext = cm + 128
    cj = cm // 128
    devices = n_gx * n_gy
    cap = resist_ref.shape[0] * 128 // devices
    jpd = cell_ref.shape[1]
    mwide = blocks * cm + cm // 2 + 128
    twide = blocks * cm + cm // 2
    gx, gy = lax.axis_index("gx"), lax.axis_index("gy")
    last_x, last_y = n_gx - 1, n_gy - 1

    def chunk_of(k):
        return lax.rem(gy + k, n_gy)

    def chunk_copies(k):
        cols = pl.ds(pl.multiple_of(chunk_of(k) * cm, cm), cm)
        return (
            pltpu.make_async_copy(temp_ref.at[:, :, cols], tbuf.at[k], load_sem.at[0, k]),
            pltpu.make_async_copy(heat_ref.at[:, :, cols], hbuf.at[k], load_sem.at[1, k]),
        )

    def mw_copies():
        return [
            pltpu.make_async_copy(
                ref, mw.at[i, pl.ds(0, rm), pl.ds(0, cm)], aux_sem.at[i]
            )
            for i, ref in enumerate((mod_ref, prev_ref))
        ]

    for copy in mw_copies():
        copy.start()

    @pl.loop(0, n_gy)
    def _(k):
        for copy in chunk_copies(k):
            copy.start()

    @pl.when(gy == last_y)
    def _():
        col_r[0] = jnp.zeros_like(col_r[0])

    @pl.when(gy == 0)
    def _():
        col_r[1] = jnp.zeros_like(col_r[1])

    @pl.when(gx == last_x)
    def _():
        row_r[0] = jnp.zeros_like(row_r[0])
        cross_r[0] = jnp.zeros_like(cross_r[0])

    @pl.when(gx == 0)
    def _():
        row_r[1] = jnp.zeros_like(row_r[1])
        cross_r[1] = jnp.zeros_like(cross_r[1])

    barrier = pltpu.get_barrier_semaphore()

    @pl.loop(1, n_gy)
    def _(d):
        pl.semaphore_signal(
            barrier, inc=1, device_id=(gx, lax.rem(gy + d, n_gy)), device_id_type=MESH
        )

    @pl.loop(1, n_gx)
    def _(d):
        pl.semaphore_signal(
            barrier, inc=1, device_id=(lax.rem(gx + d, n_gx), gy), device_id_type=MESH
        )

    @pl.when(gx < last_x)
    def _():
        pl.semaphore_signal(barrier, inc=1, device_id=(gx + 1, 0), device_id_type=MESH)

    @pl.when(gx > 0)
    def _():
        pl.semaphore_signal(
            barrier, inc=1, device_id=(gx - 1, last_y), device_id_type=MESH
        )

    lat = [lat_ref[i] for i in range(layers)]
    ver = [ver_ref[i] for i in range(layers - 1)]
    wei = [wei_ref[i] for i in range(layers)]
    fields = [
        layer_weights(lat, ver, wei),
        layer_weights(lat, ver, [None] * (layers - 1) + [1.0]),
    ]

    zero_cols = jnp.zeros((tr, 128), F32)
    for f in range(2):
        for p in range(3):
            sums[f, p, :, 0:128] = zero_cols
            sums[f, p, :, columns + 128 : columns + 256] = zero_cols

    lane8 = iota((8, 128), 1)
    for copy in mw_copies():
        copy.wait()
    for i in range(2):
        to_left = jnp.zeros((8, 128), F32)
        to_right = jnp.zeros((8, 128), F32)
        for b in range(rm // 8):
            here = (lane8 >= 4 * b) & (lane8 < 4 * b + 4)
            lo = mw[i, 8 * b : 8 * b + 8, 0:128]
            hi = mw[i, 8 * b : 8 * b + 8, cm - 128 : cm]
            to_left = jnp.where(here, pltpu.roll(lo, 4 * b, 1), to_left)
            to_right = jnp.where(here, pltpu.roll(hi, (4 * b + 4) % 128, 1), to_right)
        col_s[0, i] = to_left
        col_s[1, i] = to_right

    greeted = n_gy - 1 + n_gx - 1
    more_up = jnp.where((gy == 0) & (gx > 0), n_gy, 0)
    more_down = jnp.where((gy == last_y) & (gx < last_x), n_gy, 0)
    pl.semaphore_wait(barrier, greeted + more_up + more_down)

    def col_copy(side, to):
        return pltpu.make_async_remote_copy(
            src_ref=col_s.at[side],
            dst_ref=col_r.at[side],
            send_sem=col_ss.at[side],
            recv_sem=col_rs.at[side],
            device_id=(gx, to),
            device_id_type=MESH,
        )

    def row_copy(side, to):
        return pltpu.make_async_remote_copy(
            src_ref=row_s.at[side],
            dst_ref=row_r.at[side],
            send_sem=row_ss.at[side],
            recv_sem=row_rs.at[side],
            device_id=(to, gy),
            device_id_type=MESH,
        )

    @pl.when(gy > 0)
    def _():
        col_copy(0, gy - 1).start()

    @pl.when(gy < last_y)
    def _():
        col_copy(1, gy + 1).start()

    def layer_sums(k):
        for copy in chunk_copies(k):
            copy.wait()
        base = 128 + chunk_of(k) * cm
        for j in range(cj):
            lanes = slice(j * 128, j * 128 + 128)
            acc = [[None] * 3, [None] * 3]
            for l in range(layers):
                t, h = tbuf[k, l, :, lanes], hbuf[k, l, :, lanes]
                for f in range(2):
                    for p in range(3):
                        a, b = fields[f][p]
                        for c, x in ((a[l], t), (b[l], h)):
                            if c is not None:
                                term = c * x
                                acc[f][p] = (
                                    term if acc[f][p] is None else acc[f][p] + term
                                )
            where = pl.ds(pl.multiple_of(base + j * 128, 128), 128)
            for f in range(2):
                for p in range(3):
                    sums[f, p, :, where] = acc[f][p]

    wide = cm + 256
    crow = tr + 8

    def neighbours(x):
        r, c = x.shape
        return (
            pltpu.roll(x, 1, 0)
            + pltpu.roll(x, r - 1, 0)
            + pltpu.roll(x, 1, 1)
            + pltpu.roll(x, c - 1, 1)
            - 4.0 * x
        )

    sub8 = iota((8, cm // 2), 0)

    def contribution(f, c):
        window = pl.ds(pl.multiple_of(c * cm, cm), wide)
        zero = jnp.zeros((8, wide), F32)
        p0, p1, p2 = (
            jnp.concatenate([sums[f, p, :, window], zero], axis=0) for p in range(3)
        )
        q = p1 + neighbours(p2)
        col = c * cm - 128 + iota((crow, wide), 1)
        row = iota((crow, wide), 0)
        panel = (col >= 0) & (col < columns)
        panel = panel & ((row < tr + 4) | (gx > 0) | (gy > 0))
        panel = panel & (
            (row < tr) | (row >= tr + 4) | (gx < last_x) | (gy < last_y)
        )
        q = jnp.where(panel, q, 0.0)
        out = p0 + neighbours(q)
        main = out[:, 128 : 128 + cm]
        lane = iota((crow, 128), 1)
        halo = jnp.where(lane < 64, out[:, 128 + cm :], out[:, 0:128])
        return main, halo

    def write_message(ref, main, halo):
        for b in range(blocks):
            ref[:, b * cm : b * cm + cm] = main[8 * b : 8 * b + 8]
        edge = main[tr:]
        half = cm // 2
        at = blocks * cm
        ref[:, at : at + half] = jnp.where(
            (sub8 < 2) | (sub8 >= 6), edge[:, :half], pltpu.roll(edge[:, half:], 4, 0)
        )
        if halo is not None:
            packed = halo[0:8]
            for b in range(1, blocks + 1):
                here = (lane8 >= 8 * b - 2) & (lane8 < 8 * b + 2)
                packed = jnp.where(
                    here, pltpu.roll(halo[8 * b : 8 * b + 8], 8 * b, 1), packed
                )
            ref[:, at + half : at + half + 128] = packed

    def msg_copy(f, k):
        cols = pl.ds(0, mwide if f == 0 else twide)
        return pltpu.make_async_remote_copy(
            src_ref=msg_s.at[f, k, :, cols],
            dst_ref=msg_r.at[f, gy, :, cols],
            send_sem=msg_ss.at[f, k],
            recv_sem=msg_rs.at[f, gy],
            device_id=(gx, chunk_of(k)),
            device_id_type=MESH,
        )

    def msg_arrival(f, s):
        cols = pl.ds(0, mwide if f == 0 else twide)
        return pltpu.make_async_remote_copy(
            src_ref=msg_s.at[f, 0, :, cols],
            dst_ref=msg_r.at[f, s, :, cols],
            send_sem=msg_ss.at[f, 0],
            recv_sem=msg_rs.at[f, s],
            device_id=(gx, s),
            device_id_type=MESH,
        )

    def cross_copy(side, f, k):
        return pltpu.make_async_remote_copy(
            src_ref=cross_s.at[f, k],
            dst_ref=cross_r.at[side, f],
            send_sem=cross_ss.at[f, k],
            recv_sem=cross_rs.at[side, f],
            device_id=(gx - 1 if side == 0 else gx + 1, chunk_of(k)),
            device_id_type=MESH,
        )

    sends_up = (gy == 0) & (gx > 0)
    sends_down = (gy == last_y) & (gx < last_x)
    sub_e = iota((8, ext), 0)

    def finish(f, k, own):
        main, halo = contribution(f, chunk_of(k))

        @pl.when(sends_up)
        def _():
            block = jnp.concatenate([main, halo], axis=1)
            cross_s[f, k] = jnp.where(sub_e < 4, block[0:8], block[tr:])
            cross_copy(0, f, k).start()

        @pl.when(sends_down)
        def _():
            block = jnp.concatenate([main, halo], axis=1)
            cross_s[f, k] = jnp.where(sub_e >= 4, block[tr - 8 : tr], block[tr:])
            cross_copy(1, f, k).start()

        if own:
            write_message(msg_r.at[f, gy], main, halo if f == 0 else None)
        else:
            write_message(msg_s.at[f, k], main, halo if f == 0 else None)
            msg_copy(f, k).start()

    layer_sums(0)
    layer_sums(1)

    @pl.loop(2, n_gy + 1)
    def _(k):
        @pl.when(k < n_gy)
        def _():
            layer_sums(k)

        finish(0, k - 1, False)

    finish(0, 0, True)

    @pl.when(gy < last_y)
    def _():
        col_copy(0, gy).wait_recv()

    @pl.when(gy > 0)
    def _():
        col_copy(1, gy).wait_recv()

    for i in range(2):
        right, left = col_r[0, i], col_r[1, i]
        for b in range(rm // 8):
            mw[i, 8 * b : 8 * b + 8, cm:ext] = jnp.where(
                lane8 < 64,
                pltpu.roll(right, (128 - 4 * b) % 128, 1),
                pltpu.roll(left, (256 - 4 * b - 4) % 128, 1),
            )
        row_s[0, i] = mw[i, 0:8, :]
        row_s[1, i] = mw[i, rm - 8 : rm, :]

    @pl.when(gx > 0)
    def _():
        row_copy(0, gx - 1).start()

    @pl.when(gx < last_x)
    def _():
        row_copy(1, gx + 1).start()

    @pl.loop(1, n_gy)
    def _(k):
        finish(1, k, False)

    finish(1, 0, True)

    aux = (
        pltpu.make_async_copy(cell_ref, inc_of.at[0], aux_sem.at[2]),
        pltpu.make_async_copy(owner_ref, inc_of.at[1], aux_sem.at[3]),
    )
    for copy in aux:
        copy.start()
    state = (
        pltpu.make_async_copy(strain_ref, strain_out, aux_sem.at[4]),
        pltpu.make_async_copy(resist_ref, resist_out, aux_sem.at[5]),
    )
    for copy in state:
        copy.start()
    for copy in aux:
        copy.wait()
    jb = 256
    upper = (iota((jb, jb), 0) < iota((jb, jb), 1)).astype(F32).astype(BF16)
    own_rows = iota((devices, jb), 0)
    cell_rows = iota((rm, jb), 0)
    carry = jnp.zeros((devices, 1), F32)
    shift_c = cm.bit_length() - 1
    shift_y = n_gy.bit_length() - 1
    for i in range(jpd // jb):
        blk = slice(i * jb, i * jb + jb)
        cells, owner = inc_of[0, :, blk], inc_of[1, :, blk]
        row = lax.shift_right_logical(cells, shift_c)
        oh_row[:, blk] = (cell_rows == row).astype(F32).astype(BF16)
        place = (owner & (n_gy - 1)) * n_gx + lax.shift_right_logical(owner, shift_y)
        oh = (own_rows == place).astype(F32)
        oh_own[:, blk] = oh.astype(BF16)
        before = jnp.dot(oh.astype(BF16), upper, preferred_element_type=F32)
        slot_of[:, blk] = jnp.sum(oh * (before + carry), axis=0, keepdims=True)
        carry = carry + jnp.sum(oh, axis=1, keepdims=True)

    @pl.when(gx < last_x)
    def _():
        row_copy(0, gx).wait_recv()

    @pl.when(gx > 0)
    def _():
        row_copy(1, gx).wait_recv()

    for i in range(2):
        mw[i, rm:nrow, :] = jnp.where(sub_e < 4, row_r[0, i], row_r[1, i])

    step = next(r for r in (24, 40, 88, 8) if nrow % r == 0)

    def around(ref, start):
        rows = pl.ds(pl.multiple_of(start, 8), step)
        above = pl.ds(pl.multiple_of(lax.rem(start + nrow - 8, nrow), 8), 8)
        below = pl.ds(pl.multiple_of(lax.rem(start + step, nrow), 8), 8)
        mid = ref[rows, :]
        tall = jnp.concatenate([ref[above, :], mid, ref[below, :]], axis=0)
        return (
            mid,
            pltpu.roll(tall, 1, 0)[8 : 8 + step],
            pltpu.roll(tall, step + 15, 0)[8 : 8 + step],
            pltpu.roll(mid, 1, 1),
            pltpu.roll(mid, ext - 1, 1),
        )

    col_e = iota((step, ext), 1)
    col_ok = (col_e < cm) | ((col_e < cm + 64) & (gy < last_y)) | ((col_e >= cm + 64) & (gy > 0))

    @pl.loop(0, nrow // step)
    def _(i):
        start = i * step
        mid, *near = around(mw.at[0], start)
        row = start + iota((step, ext), 0)
        ok = (row < rm) | ((row < rm + 4) & (gx < last_x)) | ((row >= rm + 4) & (gx > 0))
        faces = [0.5 * (mid + x) for x in near]
        denom = stiffness + faces[0] + faces[1] + faces[2] + faces[3]
        inv = jnp.where(ok & col_ok, 1.0 / denom, 0.0)
        rows = pl.ds(pl.multiple_of(start, 8), step)
        for n, face in enumerate(faces):
            coef[n, rows, :] = face * inv
        coef[4, rows, :] = inv

    def arrive(f):
        @pl.loop(1, n_gy)
        def _(d):
            msg_arrival(f, lax.rem(gy + d, n_gy)).wait_recv()

        @pl.when(gx < last_x)
        def _():
            cross_copy(0, f, 0).wait_recv()

        @pl.when(gx > 0)
        def _():
            cross_copy(1, f, 0).wait_recv()

        half = cm // 2
        at = blocks * cm
        edges[0] = cross_r[1, f]
        edges[n_gy + 1] = cross_r[0, f]

        @pl.loop(0, n_gy)
        def _(s):
            both = msg_r[f, s, :, at : at + half]
            edges[s + 1, :, 0:half] = both
            edges[s + 1, :, half:cm] = pltpu.roll(both, 4, 0)
            if f == 0:
                packed = msg_r[f, s, :, at + half : at + half + 128]
                edges[s + 1, :, cm:ext] = pltpu.roll(packed, 128 - 8 * blocks, 1)

    def edge_sum(s, lanes):
        sub = iota((8, lanes.stop - lanes.start), 0)
        first = jnp.where(sub < 2, edges[s, :, lanes], 0.0)
        final = jnp.where(sub >= 6, edges[s + 2, :, lanes], 0.0)
        return first, final

    arrive(0)
    whole = slice(0, ext)

    @pl.loop(0, n_gy)
    def _(s):
        first, final = edge_sum(s, whole)
        packed = msg_r[0, s, :, twide : twide + 128]
        for b in range(blocks):
            halo = packed if b == 0 else pltpu.roll(packed, 128 - 8 * b, 1)
            x = jnp.concatenate([msg_r[0, s, :, b * cm : b * cm + cm], halo], axis=1)
            if b == 0:
                x = x + first
            if b == blocks - 1:
                x = x + final
            rows = pl.ds(pl.multiple_of(s * tr + 8 * b, 8), 8)
            load[rows, :] = x * coef[4, rows, :]

    load[rm:nrow, :] = coef[4, rm:nrow, :] * jnp.where(
        sub_e < 4, edges[n_gy] + edges[n_gy + 1], edges[1] + edges[0]
    )

    for src, dst in ((mw.at[1], wbuf.at[0]), (wbuf.at[0], wbuf.at[1]), (wbuf.at[1], wbuf.at[0])):

        @pl.loop(0, nrow // step)
        def _(i):
            start = i * step
            _mid, *near = around(src, start)
            rows = pl.ds(pl.multiple_of(start, 8), step)
            total = load[rows, :]
            for n, x in enumerate(near):
                total = total + coef[n, rows, :] * x
            dst[rows, :] = total

    result = pltpu.make_async_copy(
        wbuf.at[0, pl.ds(0, rm), pl.ds(0, cm)], warp_out, out_sem
    )
    result.start()

    def field_to(j, x):
        hi, lo = split(x.T)
        ft_hi[j * 128 : j * 128 + 128, :] = hi
        ft_lo[j * 128 : j * 128 + 128, :] = lo

    col_rows = iota((cm, jb), 0)

    def at_joints(to_ref):
        @pl.loop(0, jpd // jb)
        def _(i):
            blk = pl.ds(pl.multiple_of(i * jb, jb), jb)
            oh = oh_row[:, blk]
            got = jnp.dot(ft_hi[...], oh, preferred_element_type=F32) + jnp.dot(
                ft_lo[...], oh, preferred_element_type=F32
            )
            col = inc_of[0, :, blk] & (cm - 1)
            to_ref[:, blk] = jnp.sum(
                jnp.where(col_rows == col, got, 0.0), axis=0, keepdims=True
            )

    for j in range(cj):
        lanes = slice(j * 128, j * 128 + 128)
        field_to(j, wbuf[0, 0:rm, lanes] - mw[1, 0:rm, lanes])
    at_joints(theta_of.at[0])

    arrive(1)
    inner = slice(0, cm)

    @pl.loop(0, n_gy)
    def _(s):
        first, final = edge_sum(s, inner)
        for b in range(blocks):
            x = msg_r[1, s, :, b * cm : b * cm + cm]
            if b == 0:
                x = x + first
            if b == blocks - 1:
                x = x + final
            rows = pl.ds(pl.multiple_of(s * tr + 8 * b, 8), 8)
            top[rows, :] = x

    for j in range(cj):
        field_to(j, top[:, j * 128 : j * 128 + 128])
    at_joints(theta_of.at[1])

    kk = iota((128, jb), 0)
    total = jnp.zeros((devices, 128), F32)
    for i in range(jpd // jb):
        blk = slice(i * jb, i * jb + jb)
        rank = slot_of[:, blk].astype(jnp.int32)
        value = jnp.where(kk < cap, theta_of[0, :, blk], theta_of[1, :, blk])
        here = (kk == rank) | (kk == rank + cap)
        value = jnp.where(here, value, (kk == 2 * cap).astype(F32))
        hi, lo = split(value)
        oh = oh_own[:, blk]
        for part in (hi, lo):
            total = total + lax.dot_general(
                oh, part, (((1,), (1,)), ((), ())), preferred_element_type=F32
            )
    for y in range(n_gy):
        out1_s[y] = total[y * n_gx : y * n_gx + n_gx]

    def one_copy(d):
        to = lax.rem(gy + d, n_gy)
        return pltpu.make_async_remote_copy(
            src_ref=out1_s.at[to],
            dst_ref=out1_r.at[gy],
            send_sem=one_ss.at[d],
            recv_sem=one_rs.at[gy],
            device_id=(gx, to),
            device_id_type=MESH,
        )

    def one_arrival(s):
        return pltpu.make_async_remote_copy(
            src_ref=out1_s.at[s],
            dst_ref=out1_r.at[s],
            send_sem=one_ss.at[0],
            recv_sem=one_rs.at[s],
            device_id=(gx, s),
            device_id_type=MESH,
        )

    def two_copy(d):
        to = lax.rem(gx + d, n_gx)
        return pltpu.make_async_remote_copy(
            src_ref=out2_s.at[to],
            dst_ref=out2_r.at[gx],
            send_sem=two_ss.at[d],
            recv_sem=two_rs.at[gx],
            device_id=(to, gy),
            device_id_type=MESH,
        )

    def two_arrival(s):
        return pltpu.make_async_remote_copy(
            src_ref=out2_s.at[s],
            dst_ref=out2_r.at[s],
            send_sem=two_ss.at[0],
            recv_sem=two_rs.at[s],
            device_id=(s, gy),
            device_id_type=MESH,
        )

    @pl.loop(1, n_gy)
    def _(d):
        one_copy(d).start()

    out1_r[gy] = out1_s[gy]

    @pl.loop(1, n_gy)
    def _(d):
        one_arrival(lax.rem(gy + d, n_gy)).wait_recv()

    for x in range(n_gx):
        for y in range(n_gy):
            out2_s[x, y : y + 1, :] = out1_r[y, x : x + 1, :]

    @pl.loop(1, n_gx)
    def _(d):
        two_copy(d).start()

    out2_r[gx] = out2_s[gx]

    @pl.loop(1, n_gx)
    def _(d):
        two_arrival(lax.rem(gx + d, n_gx)).wait_recv()

    for copy in state:
        copy.wait()

    groups = devices // 8
    per = 8 * cap // 128
    flat = out2_r[...].reshape(groups, 8, 128)
    parts = [flat[:, i, :] for i in range(8)]
    counts = [jnp.broadcast_to(p[:, 2 * cap : 2 * cap + 1], (groups, 128)) for p in parts]
    lane = iota((groups, 128), 1)
    for m in range(per):
        inc = theta = jnp.zeros((groups, 128), F32)
        live = jnp.zeros((groups, 128), F32)
        for i in range(8):
            lo, hi = max(i * cap, m * 128), min((i + 1) * cap, m * 128 + 128)
            if lo >= hi:
                continue
            here = (lane >= lo - m * 128) & (lane < hi - m * 128)
            shift = (i * cap - m * 128) % 128
            inc = jnp.where(here, pltpu.roll(parts[i], shift, 1), inc)
            theta = jnp.where(here, pltpu.roll(parts[i], (shift - cap) % 128, 1), theta)
            slot = (lane + (m * 128 - i * cap)).astype(F32)
            live = jnp.where(here, jnp.where(slot < counts[i], 1.0, 0.0), live)
        rows = pl.ds(m, groups, stride=per)
        total0, inelastic, resist = (
            strain_out[0, rows, :],
            strain_out[1, rows, :],
            resist_out[rows, :],
        )
        total_new = total0 + inc
        arrhen = jnp.exp(2.0 - 2.0 / (1.0 + 0.1 * theta * theta))
        arg = shear_mod * (total_new - inelastic) / resist
        hyper = jnp.exp(arg - LN2) - jnp.exp(-arg - LN2)
        rate = rate_scale * arrhen * hyper * jnp.abs(hyper)
        size = jnp.abs(rate)
        target = sat_level * jnp.exp(sat_power * jnp.log(1.0 + size / arrhen))
        resist_new = resist + harden * (1.0 - resist / target) * size
        keep = live > 0.5
        strain_out[0, rows, :] = jnp.where(keep, total_new, total0)
        strain_out[1, rows, :] = jnp.where(keep, inelastic + rate, inelastic)
        resist_out[rows, :] = jnp.where(keep, resist_new, resist)

    result.wait()

    @pl.when(gy > 0)
    def _():
        col_copy(0, gy - 1).wait_send()

    @pl.when(gy < last_y)
    def _():
        col_copy(1, gy + 1).wait_send()

    @pl.when(gx > 0)
    def _():
        row_copy(0, gx - 1).wait_send()

    @pl.when(gx < last_x)
    def _():
        row_copy(1, gx + 1).wait_send()

    for f in range(2):

        @pl.loop(1, n_gy)
        def _(k):
            msg_copy(f, k).wait_send()

        @pl.when(sends_up)
        def _():
            @pl.loop(0, n_gy)
            def _(k):
                cross_copy(0, f, k).wait_send()

        @pl.when(sends_down)
        def _():
            @pl.loop(0, n_gy)
            def _(k):
                cross_copy(1, f, k).wait_send()

    @pl.loop(1, n_gy)
    def _(d):
        one_copy(d).wait_send()

    @pl.loop(1, n_gx)
    def _(d):
        two_copy(d).wait_send()


def solution(mesh):
    n_gx, n_gy = mesh.shape["gx"], mesh.shape["gy"]
    devices = n_gx * n_gy

    def body(
        temp_start,
        heat_input,
        lateral,
        vertical,
        weighting,
        modulus,
        warp_prev,
        joint_cell,
        joint_owner,
        joint_strain,
        joint_resist,
    ):
        layers, tr, columns = temp_start.shape
        rm, cm = modulus.shape
        jpd = joint_cell.shape[0]
        rows = joint_resist.shape[1] // 128
        blocks = tr // 8
        mwide = blocks * cm + cm // 2 + 128
        nrow, ext = rm + 8, cm + 128
        hbm = pl.BlockSpec(memory_space=pl.ANY)
        smem = pl.BlockSpec(memory_space=pltpu.SMEM)
        vmem = pl.BlockSpec(memory_space=pltpu.VMEM)
        dma = pltpu.SemaphoreType.DMA
        scratch = [
            pltpu.VMEM((n_gy, layers, tr, cm), F32),
            pltpu.VMEM((n_gy, layers, tr, cm), F32),
            pltpu.VMEM((2, 3, tr, columns + 256), F32),
            pltpu.VMEM((2, n_gy, 8, mwide), F32),
            pltpu.VMEM((2, n_gy, 8, mwide), F32),
            pltpu.VMEM((2, n_gy, 8, ext), F32),
            pltpu.VMEM((2, 2, 8, ext), F32),
            pltpu.VMEM((2, 2, 8, 128), F32),
            pltpu.VMEM((2, 2, 8, 128), F32),
            pltpu.VMEM((2, 2, 8, ext), F32),
            pltpu.VMEM((2, 2, 8, ext), F32),
            pltpu.VMEM((2, nrow, ext), F32),
            pltpu.VMEM((2, nrow, ext), F32),
            pltpu.VMEM((5, nrow, ext), F32),
            pltpu.VMEM((nrow, ext), F32),
            pltpu.VMEM((n_gy + 2, 8, ext), F32),
            pltpu.VMEM((rm, cm), F32),
            pltpu.VMEM((rm, jpd), BF16),
            pltpu.VMEM((devices, jpd), BF16),
            pltpu.VMEM((1, jpd), F32),
            pltpu.VMEM((cm, rm), BF16),
            pltpu.VMEM((cm, rm), BF16),
            pltpu.VMEM((2, 1, jpd), jnp.int32),
            pltpu.VMEM((2, 1, jpd), F32),
            pltpu.VMEM((n_gy, n_gx, 128), F32),
            pltpu.VMEM((n_gy, n_gx, 128), F32),
            pltpu.VMEM((n_gx, n_gy, 128), F32),
            pltpu.VMEM((n_gx, n_gy, 128), F32),
            dma((2, n_gy)),
            dma((6,)),
            dma,
            dma((2,)),
            dma((2,)),
            dma((2,)),
            dma((2,)),
            dma((2, n_gy)),
            dma((2, n_gy)),
            dma((2, n_gy)),
            dma((2, 2)),
            dma((n_gy,)),
            dma((n_gy,)),
            dma((n_gx,)),
            dma((n_gx,)),
        ]
        warp, strain, resist = pl.pallas_call(
            functools.partial(kernel, n_gx, n_gy),
            out_shape=(
                jax.ShapeDtypeStruct((rm, cm), F32),
                jax.ShapeDtypeStruct((2, rows, 128), F32),
                jax.ShapeDtypeStruct((rows, 128), F32),
            ),
            in_specs=[hbm, hbm, smem, smem, smem, hbm, hbm, hbm, hbm, hbm, hbm],
            out_specs=(hbm, vmem, vmem),
            scratch_shapes=scratch,
            compiler_params=pltpu.CompilerParams(
                collective_id=0, has_side_effects=True, vmem_limit_bytes=56 * 2**20
            ),
        )(
            temp_start,
            heat_input,
            lateral,
            vertical,
            weighting,
            modulus,
            warp_prev,
            joint_cell.reshape(1, jpd),
            joint_owner.reshape(1, jpd),
            joint_strain.reshape(2, rows, 128),
            joint_resist.reshape(rows, 128),
        )
        return (
            warp,
            strain.reshape(joint_strain.shape),
            resist.reshape(joint_resist.shape),
        )

    return jax.shard_map(
        body,
        mesh=mesh,
        in_specs=(
            P(None, ("gx", "gy"), None),
            P(None, ("gx", "gy"), None),
            P(),
            P(),
            P(),
            P("gx", "gy"),
            P("gx", "gy"),
            P(("gx", "gy")),
            P(("gx", "gy"), None),
            P(None, ("gx", "gy"), None),
            P(("gx", "gy"), None),
        ),
        out_specs=(P("gx", "gy"), P(None, ("gx", "gy"), None), P(("gx", "gy"), None)),
        check_vma=False,
    )
```

```python
import functools

import jax
import jax.numpy as jnp
from jax import lax
from jax.experimental import pallas as pl
from jax.experimental.pallas import tpu as pltpu
from jax.sharding import PartitionSpec as P

MESH = pl.DeviceIdType.MESH
F32 = jnp.float32
BF16 = jnp.bfloat16

stiffness = 0.2
shear_mod = 0.6
rate_scale = 0.5
sat_level = 2.5
sat_power = 0.3
harden = 2.0
LN2 = 0.6931471805599453


def iota(shape, dim):
    return lax.broadcasted_iota(jnp.int32, shape, dim)


def split(x):
    hi = x.astype(BF16)
    return hi, (x - hi.astype(F32)).astype(BF16)


def layer_weights(lat, ver, w):
    n = len(w)

    def add(x, y):
        return y if x is None else x if y is None else x + y

    def mul(x, y):
        return None if x is None else x * y

    def vert(x):
        out = []
        for l in range(n):
            keep = 1.0
            if l < n - 1:
                keep = keep - ver[l]
            if l > 0:
                keep = keep - ver[l - 1]
            total = mul(x[l], keep)
            if l > 0:
                total = add(total, mul(x[l - 1], ver[l - 1]))
            if l < n - 1:
                total = add(total, mul(x[l + 1], ver[l]))
            out.append(total)
        return out

    u = vert(w)
    wd = [mul(x, d) for x, d in zip(w, lat)]
    a0 = vert(u)
    a1 = [add(mul(x, d), y) for x, d, y in zip(u, lat, vert(wd))]
    a2 = [mul(x, d) for x, d in zip(wd, lat)]
    b0 = [add(x, y) for x, y in zip(u, w)]
    return (a0, b0), (a1, wd), (a2, [None] * n)


def kernel(
    n_gx,
    n_gy,
    cap,
    temp_ref,
    heat_ref,
    lat_ref,
    ver_ref,
    wei_ref,
    mod_ref,
    prev_ref,
    cell_ref,
    owner_ref,
    warp_out,
    rows_out,
    tbuf,
    hbuf,
    sums,
    msg_s,
    msg_r,
    cross_s,
    cross_r,
    edge_s,
    edge_r,
    col_s,
    col_r,
    mw,
    wbuf,
    coef,
    load,
    f_hi,
    f_lo,
    oh_col,
    oh_own,
    slot_of,
    owner_of,
    cell_r,
    reply_s,
    reply_r,
    inc_of,
    theta_of,
    out1_s,
    out1_r,
    out2_s,
    load_sem,
    mw_sem,
    aux_sem,
    out_sem,
    col_ss,
    col_rs,
    row_ss,
    row_rs,
    msg_ss,
    msg_rs,
    cross_ss,
    cross_rs,
    edge_ss,
    edge_rs,
    ask_ss,
    ask_rs,
    reply_ss,
    reply_rs,
    one_ss,
    one_rs,
    two_ss,
    two_rs,
):
    layers, tr, columns = temp_ref.shape
    rm, cm = mod_ref.shape
    blocks = tr // 8
    ext = cm + 128
    cj = cm // 128
    devices = n_gx * n_gy
    jpd = cell_ref.shape[1]
    gx, gy = lax.axis_index("gx"), lax.axis_index("gy")
    last_x, last_y = n_gx - 1, n_gy - 1
    base = 16
    below = base + rm

    def remote(src, dst, ss, rs, to):
        return pltpu.make_async_remote_copy(
            src_ref=src,
            dst_ref=dst,
            send_sem=ss,
            recv_sem=rs,
            device_id=to,
            device_id_type=MESH,
        )

    def chunk_of(k):
        return lax.rem(gy + k, n_gy)

    def chunk_copies(k):
        cols = pl.ds(pl.multiple_of(chunk_of(k) * cm, cm), cm)
        return (
            pltpu.make_async_copy(temp_ref.at[:, :, cols], tbuf.at[k], load_sem.at[0, k]),
            pltpu.make_async_copy(heat_ref.at[:, :, cols], hbuf.at[k], load_sem.at[1, k]),
        )

    def mw_copies():
        return [
            pltpu.make_async_copy(
                ref.at[:, pl.ds(j * 128, 128)],
                mw.at[i, j, pl.ds(base, rm), :],
                mw_sem.at[i, j],
            )
            for i, ref in enumerate((mod_ref, prev_ref))
            for j in range(cj)
        ]

    aux = (
        pltpu.make_async_copy(cell_ref, cell_r.at[gy], aux_sem.at[0]),
        pltpu.make_async_copy(owner_ref, owner_of, aux_sem.at[1]),
    )

    @pl.loop(0, 3)
    def _(k):
        for copy in chunk_copies(k):
            copy.start()

    for copy in mw_copies():
        copy.start()
    for copy in aux:
        copy.start()

    @pl.loop(3, n_gy)
    def _(k):
        for copy in chunk_copies(k):
            copy.start()

    @pl.when(gy == last_y)
    def _():
        col_r[0] = jnp.zeros_like(col_r[0])

    @pl.when(gy == 0)
    def _():
        col_r[1] = jnp.zeros_like(col_r[1])

    zero8 = jnp.zeros((8, 128), F32)

    @pl.when(gx == last_x)
    def _():
        for i in range(2):
            for j in range(cj + 1):
                mw[i, j, below : below + 8, :] = zero8
        cross_r[0] = jnp.zeros_like(cross_r[0])
        edge_r[0] = jnp.zeros_like(edge_r[0])

    @pl.when(gx == 0)
    def _():
        for i in range(2):
            for j in range(cj + 1):
                mw[i, j, base - 8 : base, :] = zero8
        cross_r[1] = jnp.zeros_like(cross_r[1])
        edge_r[1] = jnp.zeros_like(edge_r[1])

    barrier = pltpu.get_barrier_semaphore()

    @pl.loop(1, n_gy)
    def _(d):
        pl.semaphore_signal(
            barrier, inc=1, device_id=(gx, lax.rem(gy + d, n_gy)), device_id_type=MESH
        )

    @pl.loop(1, n_gx)
    def _(d):
        pl.semaphore_signal(
            barrier, inc=1, device_id=(lax.rem(gx + d, n_gx), gy), device_id_type=MESH
        )

    @pl.when(gx < last_x)
    def _():
        pl.semaphore_signal(barrier, inc=1, device_id=(gx + 1, 0), device_id_type=MESH)

    @pl.when(gx > 0)
    def _():
        pl.semaphore_signal(
            barrier, inc=1, device_id=(gx - 1, last_y), device_id_type=MESH
        )

    lat = [lat_ref[i] for i in range(layers)]
    ver = [ver_ref[i] for i in range(layers - 1)]
    wei = [wei_ref[i] for i in range(layers)]
    fields = [
        layer_weights(lat, ver, wei),
        layer_weights(lat, ver, [None] * (layers - 1) + [1.0]),
    ]

    zero_cols = jnp.zeros((tr, 128), F32)
    for f in range(2):
        for p in range(3):
            sums[f, p, :, 0:128] = zero_cols
            sums[f, p, :, columns + 128 : columns + 256] = zero_cols
    for j in range(cj + 1):
        for rows in (slice(0, 8), slice(below + 8, below + 16)):
            for ref in (mw.at[0], mw.at[1], wbuf.at[0], wbuf.at[1]):
                ref[j, rows, :] = zero8

    def layer_sums(k):
        for copy in chunk_copies(k):
            copy.wait()
        start = 128 + chunk_of(k) * cm
        for j in range(cj):
            lanes = slice(j * 128, j * 128 + 128)
            acc = [[None] * 3, [None] * 3]
            for l in range(layers):
                t, h = tbuf[k, l, :, lanes], hbuf[k, l, :, lanes]
                for f in range(2):
                    for p in range(3):
                        a, b = fields[f][p]
                        for c, x in ((a[l], t), (b[l], h)):
                            if c is not None:
                                term = c * x
                                acc[f][p] = (
                                    term if acc[f][p] is None else acc[f][p] + term
                                )
            where = pl.ds(pl.multiple_of(start + j * 128, 128), 128)
            for f in range(2):
                for p in range(3):
                    sums[f, p, :, where] = acc[f][p]

    wide = cm + 256
    crow = tr + 8

    def neighbours(x):
        r, c = x.shape
        return (
            pltpu.roll(x, 1, 0)
            + pltpu.roll(x, r - 1, 0)
            + pltpu.roll(x, 1, 1)
            + pltpu.roll(x, c - 1, 1)
            - 4.0 * x
        )

    def contribution(f, c):
        window = pl.ds(pl.multiple_of(c * cm, cm), wide)
        zero = jnp.zeros((8, wide), F32)
        p0, p1, p2 = (
            jnp.concatenate([sums[f, p, :, window], zero], axis=0) for p in range(3)
        )
        q = p1 + neighbours(p2)
        col = c * cm - 128 + iota((crow, wide), 1)
        row = iota((crow, wide), 0)
        panel = (col >= 0) & (col < columns)
        panel = panel & ((row < tr + 4) | (gx > 0) | (gy > 0))
        panel = panel & (
            (row < tr) | (row >= tr + 4) | (gx < last_x) | (gy < last_y)
        )
        q = jnp.where(panel, q, 0.0)
        out = p0 + neighbours(q)
        main = out[:, 128 : 128 + cm]
        lane = iota((crow, 128), 1)
        halo = jnp.where(lane < 64, out[:, 128 + cm :], out[:, 0:128])
        return main, halo

    lane8 = iota((8, 128), 1)
    sub8 = iota((8, 128), 0)
    sub_h = iota((8, cm // 2), 0)
    sub_e = iota((8, ext), 0)
    half = cm // 2
    at = blocks * cm

    def write_message(ref, main, halo):
        for b in range(blocks):
            ref[:, b * cm : b * cm + cm] = main[8 * b : 8 * b + 8]
        edge = main[tr:]
        ref[:, at : at + half] = jnp.where(
            (sub_h < 2) | (sub_h >= 6), edge[:, :half], pltpu.roll(edge[:, half:], 4, 0)
        )
        packed = halo[0:8]
        for b in range(1, blocks + 1):
            here = (lane8 >= 8 * b - 2) & (lane8 < 8 * b + 2)
            packed = jnp.where(
                here, pltpu.roll(halo[8 * b : 8 * b + 8], 8 * b, 1), packed
            )
        ref[:, at + half : at + half + 128] = packed

    def msg_copy(k):
        return remote(
            msg_s.at[k], msg_r.at[gy], msg_ss.at[k], msg_rs.at[gy], (gx, chunk_of(k))
        )

    def msg_arrival(s):
        return remote(msg_s.at[0], msg_r.at[s], msg_ss.at[0], msg_rs.at[s], (gx, s))

    def beyond(side):
        return gx - 1 if side == 0 else gx + 1

    def cross_copy(side, k):
        return remote(
            cross_s.at[k],
            cross_r.at[side],
            cross_ss.at[k],
            cross_rs.at[side],
            (beyond(side), chunk_of(k)),
        )

    def edge_copy(side, k):
        return remote(
            edge_s.at[k],
            edge_r.at[side],
            edge_ss.at[k],
            edge_rs.at[side],
            (beyond(side), chunk_of(k)),
        )

    sends_up = (gy == 0) & (gx > 0)
    sends_down = (gy == last_y) & (gx < last_x)

    def prepare(k, to_ref):
        main, halo = contribution(0, chunk_of(k))
        write_message(to_ref, main, halo)

        @pl.when(sends_up)
        def _():
            block = jnp.concatenate([main, halo], axis=1)
            cross_s[k] = jnp.where(sub_e < 4, block[0:8], block[tr:])

        @pl.when(sends_down)
        def _():
            block = jnp.concatenate([main, halo], axis=1)
            cross_s[k] = jnp.where(sub_e >= 4, block[tr - 8 : tr], block[tr:])

    def send_cross(copy_of, k):
        @pl.when(sends_up)
        def _():
            copy_of(0, k).start()

        @pl.when(sends_down)
        def _():
            copy_of(1, k).start()

    layer_sums(0)
    layer_sums(1)
    layer_sums(2)
    prepare(1, msg_s.at[1])

    greeted = n_gy - 1 + n_gx - 1
    more_up = jnp.where((gy == 0) & (gx > 0), n_gy, 0)
    more_down = jnp.where((gy == last_y) & (gx < last_x), n_gy, 0)
    pl.semaphore_wait(barrier, greeted + more_up + more_down)

    msg_copy(1).start()
    send_cross(cross_copy, 1)

    def ask_copy(d):
        return remote(
            cell_ref, cell_r.at[gy], ask_ss.at[d], ask_rs.at[gy], (gx, chunk_of(d))
        )

    def ask_arrival(s):
        return remote(cell_ref, cell_r.at[s], ask_ss.at[0], ask_rs.at[s], (gx, s))

    for copy in mw_copies():
        copy.wait()
    for i in range(2):
        to_left, to_right = zero8, zero8
        for b in range(rm // 8):
            here = (lane8 >= 4 * b) & (lane8 < 4 * b + 4)
            rows = slice(base + 8 * b, base + 8 * b + 8)
            to_left = jnp.where(here, pltpu.roll(mw[i, 0, rows, :], 4 * b, 1), to_left)
            to_right = jnp.where(
                here,
                pltpu.roll(mw[i, cj - 1, rows, :], (4 * b + 4) % 128, 1),
                to_right,
            )
        col_s[0, i] = to_left
        col_s[1, i] = to_right

    def col_copy(side, to):
        return remote(
            col_s.at[side], col_r.at[side], col_ss.at[side], col_rs.at[side], (gx, to)
        )

    @pl.when(gy > 0)
    def _():
        col_copy(0, gy - 1).start()

    @pl.when(gy < last_y)
    def _():
        col_copy(1, gy + 1).start()

    @pl.loop(1, n_gy)
    def _(d):
        ask_copy(d).start()

    @pl.loop(3, n_gy + 1)
    def _(k):
        @pl.when(k < n_gy)
        def _():
            layer_sums(k)

        prepare(k - 1, msg_s.at[k - 1])
        msg_copy(k - 1).start()
        send_cross(cross_copy, k - 1)

    prepare(0, msg_r.at[gy])
    send_cross(cross_copy, 0)

    @pl.when(gy < last_y)
    def _():
        col_copy(0, gy).wait_recv()

    @pl.when(gy > 0)
    def _():
        col_copy(1, gy).wait_recv()

    for i in range(2):
        right, left = col_r[0, i], col_r[1, i]
        for b in range(rm // 8):
            mw[i, cj, base + 8 * b : base + 8 * b + 8, :] = jnp.where(
                lane8 < 64,
                pltpu.roll(right, (128 - 4 * b) % 128, 1),
                pltpu.roll(left, (256 - 4 * b - 4) % 128, 1),
            )

    def row_copy(side, to):
        src = base if side == 0 else below - 8
        dst = below if side == 0 else base - 8
        return remote(
            mw.at[:, :, pl.ds(src, 8), :],
            mw.at[:, :, pl.ds(dst, 8), :],
            row_ss.at[side],
            row_rs.at[side],
            (to, gy),
        )

    @pl.when(gx > 0)
    def _():
        row_copy(0, gx - 1).start()

    @pl.when(gx < last_x)
    def _():
        row_copy(1, gx + 1).start()

    for copy in aux:
        copy.wait()

    @pl.loop(1, n_gy)
    def _(d):
        ask_arrival(lax.rem(gy + d, n_gy)).wait_recv()

    jb = 256
    shift_c = cm.bit_length() - 1
    shift_y = n_gy.bit_length() - 1
    lane_rows = iota((128, jb), 0)

    def one_hot(rows, at_row):
        return (rows == at_row).astype(F32).astype(BF16)

    def select(table, row_of, cells_ref, to_ref):
        tall = table.shape[0]
        per = tall // cj
        lhs = jnp.concatenate(split(table), axis=1)
        ids = iota((tall, jb), 0)
        for i in range(jpd // jb):
            blk = slice(i * jb, i * jb + jb)
            cells = cells_ref[:, blk]
            row = row_of(lax.shift_right_logical(cells, shift_c))
            block = lax.shift_right_logical(cells & (cm - 1), 7)
            place = jnp.where(row >= 0, block * per + row, -1)
            oh = one_hot(lane_rows, cells & 127)
            got = jnp.dot(
                lhs, jnp.concatenate([oh, oh], axis=0), preferred_element_type=F32
            )
            to_ref[:, blk] = jnp.sum(
                jnp.where(ids == place, got, 0.0), axis=0, keepdims=True
            )

    def stacked(x):
        return jnp.concatenate([x[:, j * 128 : j * 128 + 128] for j in range(cj)], axis=0)

    def near_row(row):
        q = row - gy * tr
        inside = (q >= 0) & (q < tr + 2)
        before = (q < 0) & (q >= -2)
        return jnp.where(inside, q, jnp.where(before, q + crow, -1))

    def reply_copy(k):
        return remote(
            reply_s.at[k],
            reply_r.at[gy],
            reply_ss.at[k],
            reply_rs.at[gy],
            (gx, chunk_of(k)),
        )

    def reply_arrival(s):
        return remote(
            reply_s.at[0], reply_r.at[s], reply_ss.at[0], reply_rs.at[s], (gx, s)
        )

    def answer(k, to_ref):
        main, _halo = contribution(1, chunk_of(k))

        @pl.when(sends_up | sends_down)
        def _():
            edge_s[k] = main[tr:]

        send_cross(edge_copy, k)
        select(stacked(main), near_row, cell_r.at[chunk_of(k)], to_ref)

    @pl.loop(1, n_gy)
    def _(k):
        answer(k, reply_s.at[k])
        reply_copy(k).start()

    answer(0, reply_r.at[gy])

    step = 16
    lane_s = iota((step, 128), 1)

    def around(ref, start):
        rows = pl.ds(pl.multiple_of(start, 8), step)
        mid = [ref[j, rows, :] for j in range(cj + 1)]
        up = [ref[j, pl.ds(start - 1, step), :] for j in range(cj + 1)]
        down = [ref[j, pl.ds(start + 1, step), :] for j in range(cj + 1)]
        to_r = [pltpu.roll(x, 1, 1) for x in mid]
        to_l = [pltpu.roll(x, 127, 1) for x in mid]
        left = [jnp.where(lane_s == 0, to_r[j - 1], to_r[j]) for j in range(cj + 1)]
        right = [
            jnp.where(lane_s == 127, to_l[(j + 1) % (cj + 1)], to_l[j])
            for j in range(cj + 1)
        ]
        return mid, list(zip(up, down, left, right))

    @pl.when(gx < last_x)
    def _():
        row_copy(0, gx).wait_recv()

    @pl.when(gx > 0)
    def _():
        row_copy(1, gx).wait_recv()

    halo_ok = ((lane_s < 64) & (gy < last_y)) | ((lane_s >= 64) & (gy > 0))

    @pl.loop(0, (rm + 16) // step)
    def _(i):
        start = base - 8 + i * step
        rows = pl.ds(pl.multiple_of(start, 8), step)
        mid, near = around(mw.at[0], start)
        row = start + iota((step, 128), 0)
        ok = ((row >= base) | (gx > 0)) & ((row < below) | (gx < last_x))
        for j in range(cj + 1):
            faces = [0.5 * (mid[j] + x) for x in near[j]]
            denom = stiffness + faces[0] + faces[1] + faces[2] + faces[3]
            inv = jnp.where(ok & halo_ok if j == cj else ok, 1.0 / denom, 0.0)
            for n, face in enumerate(faces):
                coef[n, j, rows, :] = face * inv
            coef[4, j, rows, :] = inv

    upper = (iota((jb, jb), 0) < iota((jb, jb), 1)).astype(F32).astype(BF16)
    own_rows = iota((devices, jb), 0)
    col_rows = iota((cm, jb), 0)
    carry = jnp.zeros((devices, 1), F32)
    for i in range(jpd // jb):
        blk = slice(i * jb, i * jb + jb)
        oh_col[:, blk] = one_hot(col_rows, cell_r[gy, :, blk] & (cm - 1))
        owner = owner_of[:, blk]
        place = (owner & (n_gy - 1)) * n_gx + lax.shift_right_logical(owner, shift_y)
        oh = (own_rows == place).astype(F32)
        oh_own[:, blk] = oh.astype(BF16)
        before = jnp.dot(oh.astype(BF16), upper, preferred_element_type=F32)
        slot_of[:, blk] = jnp.sum(oh * (before + carry), axis=0, keepdims=True)
        carry = carry + jnp.sum(oh, axis=1, keepdims=True)

    for j in range(cj + 1):
        for rows in (slice(base - 8, base), slice(below, below + 8)):
            load[j, rows, :] = zero8

    @pl.loop(0, n_gy)
    def _(d):
        s = lax.rem(gy + n_gy - d, n_gy)

        @pl.when(d > 0)
        def _():
            msg_arrival(s).wait_recv()

        packed = msg_r[s, :, at + half : at + half + 128]
        for b in range(blocks):
            rows = pl.ds(pl.multiple_of(base + s * tr + 8 * b, 8), 8)
            for j in range(cj):
                lanes = slice(b * cm + j * 128, b * cm + j * 128 + 128)
                load[j, rows, :] = msg_r[s, :, lanes] * coef[4, j, rows, :]
            halo = packed if b == 0 else pltpu.roll(packed, 128 - 8 * b, 1)
            load[cj, rows, :] = halo * coef[4, cj, rows, :]

    def add_edges(start, keep, parts):
        rows = pl.ds(pl.multiple_of(start, 8), 8)
        for j, x in enumerate(parts):
            load[j, rows, :] = load[j, rows, :] + jnp.where(
                keep, x * coef[4, j, rows, :], 0.0
            )

    for s in range(n_gy):
        both = [msg_r[s, :, at + j * 128 : at + j * 128 + 128] for j in range(cj // 2)]
        parts = both + [pltpu.roll(x, 4, 0) for x in both]
        parts.append(
            pltpu.roll(msg_r[s, :, at + half : at + half + 128], 128 - 8 * blocks, 1)
        )
        add_edges(base + (s + 1) * tr, sub8 < 2, parts)
        add_edges(base + s * tr - 8, sub8 >= 6, parts)

    @pl.when(gx < last_x)
    def _():
        cross_copy(0, 0).wait_recv()
        parts = [cross_r[0, :, j * 128 : j * 128 + 128] for j in range(cj + 1)]
        add_edges(below, sub8 < 2, parts)
        add_edges(below - 8, sub8 >= 6, parts)

    @pl.when(gx > 0)
    def _():
        cross_copy(1, 0).wait_recv()
        parts = [cross_r[1, :, j * 128 : j * 128 + 128] for j in range(cj + 1)]
        add_edges(base, sub8 < 2, parts)
        add_edges(base - 8, sub8 >= 6, parts)

    def swept(src, start, j, near):
        rows = pl.ds(pl.multiple_of(start, 8), step)
        total = load[j, rows, :]
        for n, x in enumerate(near[j]):
            total = total + coef[n, j, rows, :] * x
        return total

    for src, dst in ((mw.at[1], wbuf.at[0]), (wbuf.at[0], wbuf.at[1])):

        @pl.loop(0, (rm + 16) // step)
        def _(i):
            start = base - 8 + i * step
            _mid, near = around(src, start)
            for j in range(cj + 1):
                dst[j, pl.ds(pl.multiple_of(start, 8), step), :] = swept(
                    src, start, j, near
                )

    @pl.loop(0, rm // step)
    def _(i):
        start = base + i * step
        rows = pl.ds(pl.multiple_of(start, 8), step)
        tile_rows = pl.ds(pl.multiple_of(i * step, step), step)
        _mid, near = around(wbuf.at[1], start)
        for j in range(cj):
            lanes = slice(j * 128, j * 128 + 128)
            x = swept(wbuf.at[1], start, j, near)
            wbuf[0, j, rows, :] = x
            hi, lo = split(x - mw[1, j, rows, :])
            f_hi[tile_rows, lanes] = hi
            f_lo[tile_rows, lanes] = lo

    results = [
        pltpu.make_async_copy(
            wbuf.at[0, j, pl.ds(base, rm), :],
            warp_out.at[:, pl.ds(j * 128, 128)],
            out_sem.at[j],
        )
        for j in range(cj)
    ]
    for copy in results:
        copy.start()

    tile_ids = iota((rm, jb), 0)
    for i in range(jpd // jb):
        blk = slice(i * jb, i * jb + jb)
        oh = oh_col[:, blk]
        got = jnp.dot(f_hi[...], oh, preferred_element_type=F32) + jnp.dot(
            f_lo[...], oh, preferred_element_type=F32
        )
        row = lax.shift_right_logical(cell_r[gy, :, blk], shift_c)
        inc_of[:, blk] = jnp.sum(
            jnp.where(tile_ids == row, got, 0.0), axis=0, keepdims=True
        )

    @pl.when(gx < last_x)
    def _():
        edge_copy(0, 0).wait_recv()

    @pl.when(gx > 0)
    def _():
        edge_copy(1, 0).wait_recv()

    def outer_row(row):
        return jnp.where(row < 2, row, jnp.where(row >= rm - 2, row - (rm - 8), -1))

    sub_c = iota((8, cm), 0)
    select(
        stacked(jnp.where(sub_c < 4, edge_r[1], edge_r[0])),
        outer_row,
        cell_r.at[gy],
        theta_of,
    )

    @pl.loop(1, n_gy)
    def _(d):
        reply_arrival(lax.rem(gy + d, n_gy)).wait_recv()

    theta = theta_of[...]
    for s in range(n_gy):
        theta = theta + reply_r[s]
    theta_of[...] = theta

    kk = iota((128, jb), 0)
    total = jnp.zeros((devices, 128), F32)
    for i in range(jpd // jb):
        blk = slice(i * jb, i * jb + jb)
        rank = slot_of[:, blk].astype(jnp.int32)
        value = jnp.where(kk < cap, inc_of[:, blk], theta_of[:, blk])
        here = (kk == rank) | (kk == rank + cap)
        value = jnp.where(here, value, (kk == 2 * cap).astype(F32))
        hi, lo = split(value)
        oh = oh_own[:, blk]
        for part in (hi, lo):
            total = total + lax.dot_general(
                oh, part, (((1,), (1,)), ((), ())), preferred_element_type=F32
            )
    for y in range(n_gy):
        out1_s[y] = total[y * n_gx : y * n_gx + n_gx]

    def one_copy(d):
        to = lax.rem(gy + d, n_gy)
        return remote(
            out1_s.at[to], out1_r.at[gy], one_ss.at[d], one_rs.at[gy], (gx, to)
        )

    def one_arrival(s):
        return remote(out1_s.at[s], out1_r.at[s], one_ss.at[0], one_rs.at[s], (gx, s))

    def two_copy(d):
        to = lax.rem(gx + d, n_gx)
        return remote(
            out2_s.at[to], rows_out.at[gx], two_ss.at[d], two_rs.at[gx], (to, gy)
        )

    def two_arrival(s):
        return remote(out2_s.at[s], rows_out.at[s], two_ss.at[0], two_rs.at[s], (s, gy))

    @pl.loop(1, n_gy)
    def _(d):
        one_copy(d).start()

    out1_r[gy] = out1_s[gy]

    @pl.loop(1, n_gy)
    def _(d):
        one_arrival(lax.rem(gy + d, n_gy)).wait_recv()

    for x in range(n_gx):
        for y in range(n_gy):
            out2_s[x, y : y + 1, :] = out1_r[y, x : x + 1, :]

    @pl.loop(1, n_gx)
    def _(d):
        two_copy(d).start()

    own = pltpu.make_async_copy(out2_s.at[gx], rows_out.at[gx], aux_sem.at[2])
    own.start()

    for copy in results:
        copy.wait()

    @pl.when(gy > 0)
    def _():
        col_copy(0, gy - 1).wait_send()

    @pl.when(gy < last_y)
    def _():
        col_copy(1, gy + 1).wait_send()

    @pl.when(gx > 0)
    def _():
        row_copy(0, gx - 1).wait_send()

    @pl.when(gx < last_x)
    def _():
        row_copy(1, gx + 1).wait_send()

    @pl.loop(1, n_gy)
    def _(k):
        msg_copy(k).wait_send()
        ask_copy(k).wait_send()
        reply_copy(k).wait_send()
        one_copy(k).wait_send()

    for side, sends in ((0, sends_up), (1, sends_down)):

        @pl.when(sends)
        def _():
            @pl.loop(0, n_gy)
            def _(k):
                cross_copy(side, k).wait_send()
                edge_copy(side, k).wait_send()

    own.wait()

    @pl.loop(1, n_gx)
    def _(d):
        two_copy(d).wait_send()

    @pl.loop(1, n_gx)
    def _(d):
        two_arrival(lax.rem(gx + d, n_gx)).wait_recv()


def finish_kernel(
    warp_ref, rows_ref, strain_ref, resist_ref, warp_out, strain_out, resist_out, sem
):
    copy = pltpu.make_async_copy(warp_ref, warp_out, sem)
    copy.start()
    devices = rows_ref.shape[0]
    cap = resist_ref.shape[0] * 128 // devices
    groups = devices // 8
    per = 8 * cap // 128
    parts = [rows_ref[pl.ds(i, groups, stride=8), :] for i in range(8)]
    counts = [jnp.broadcast_to(p[:, 2 * cap : 2 * cap + 1], (groups, 128)) for p in parts]
    lane = iota((groups, 128), 1)
    for m in range(per):
        inc = theta = jnp.zeros((groups, 128), F32)
        live = jnp.zeros((groups, 128), F32)
        for i in range(8):
            lo, hi = max(i * cap, m * 128), min((i + 1) * cap, m * 128 + 128)
            if lo >= hi:
                continue
            here = (lane >= lo - m * 128) & (lane < hi - m * 128)
            shift = (i * cap - m * 128) % 128
            inc = jnp.where(here, pltpu.roll(parts[i], shift, 1), inc)
            theta = jnp.where(here, pltpu.roll(parts[i], (shift - cap) % 128, 1), theta)
            slot = (lane + (m * 128 - i * cap)).astype(F32)
            live = jnp.where(here, jnp.where(slot < counts[i], 1.0, 0.0), live)
        rows = pl.ds(m, groups, stride=per)
        total0, inelastic, resist = (
            strain_ref[0, rows, :],
            strain_ref[1, rows, :],
            resist_ref[rows, :],
        )
        total_new = total0 + inc
        arrhen = jnp.exp(2.0 - 2.0 / (1.0 + 0.1 * theta * theta))
        arg = shear_mod * (total_new - inelastic) / resist
        hyper = jnp.exp(arg - LN2) - jnp.exp(-arg - LN2)
        rate = rate_scale * arrhen * hyper * jnp.abs(hyper)
        size = jnp.abs(rate)
        target = sat_level * jnp.exp(sat_power * jnp.log(1.0 + size / arrhen))
        resist_new = resist + harden * (1.0 - resist / target) * size
        keep = live > 0.5
        strain_out[0, rows, :] = jnp.where(keep, total_new, total0)
        strain_out[1, rows, :] = jnp.where(keep, inelastic + rate, inelastic)
        resist_out[rows, :] = jnp.where(keep, resist_new, resist)
    copy.wait()


def solution(mesh):
    n_gx, n_gy = mesh.shape["gx"], mesh.shape["gy"]
    devices = n_gx * n_gy

    def body(
        temp_start,
        heat_input,
        lateral,
        vertical,
        weighting,
        modulus,
        warp_prev,
        joint_cell,
        joint_owner,
        joint_strain,
        joint_resist,
    ):
        layers, tr, columns = temp_start.shape
        rm, cm = modulus.shape
        jpd = joint_cell.shape[0]
        rows = joint_resist.shape[1] // 128
        blocks = tr // 8
        mwide = blocks * cm + cm // 2 + 128
        ext, cb, tall = cm + 128, cm // 128 + 1, rm + 32
        hbm = pl.BlockSpec(memory_space=pl.ANY)
        smem = pl.BlockSpec(memory_space=pltpu.SMEM)
        vmem = pl.BlockSpec(memory_space=pltpu.VMEM)
        dma = pltpu.SemaphoreType.DMA
        scratch = [
            pltpu.VMEM((n_gy, layers, tr, cm), F32),
            pltpu.VMEM((n_gy, layers, tr, cm), F32),
            pltpu.VMEM((2, 3, tr, columns + 256), F32),
            pltpu.VMEM((n_gy, 8, mwide), F32),
            pltpu.VMEM((n_gy, 8, mwide), F32),
            pltpu.VMEM((n_gy, 8, ext), F32),
            pltpu.VMEM((2, 8, ext), F32),
            pltpu.VMEM((n_gy, 8, cm), F32),
            pltpu.VMEM((2, 8, cm), F32),
            pltpu.VMEM((2, 2, 8, 128), F32),
            pltpu.VMEM((2, 2, 8, 128), F32),
            pltpu.VMEM((2, cb, tall, 128), F32),
            pltpu.VMEM((2, cb, tall, 128), F32),
            pltpu.VMEM((5, cb, tall, 128), F32),
            pltpu.VMEM((cb, tall, 128), F32),
            pltpu.VMEM((rm, cm), BF16),
            pltpu.VMEM((rm, cm), BF16),
            pltpu.VMEM((cm, jpd), BF16),
            pltpu.VMEM((devices, jpd), BF16),
            pltpu.VMEM((1, jpd), F32),
            pltpu.VMEM((1, jpd), jnp.int32),
            pltpu.VMEM((n_gy, 1, jpd), jnp.int32),
            pltpu.VMEM((n_gy, 1, jpd), F32),
            pltpu.VMEM((n_gy, 1, jpd), F32),
            pltpu.VMEM((1, jpd), F32),
            pltpu.VMEM((1, jpd), F32),
            pltpu.VMEM((n_gy, n_gx, 128), F32),
            pltpu.VMEM((n_gy, n_gx, 128), F32),
            pltpu.VMEM((n_gx, n_gy, 128), F32),
            dma((2, n_gy)),
            dma((2, cb - 1)),
            dma((3,)),
            dma((cb - 1,)),
            dma((2,)),
            dma((2,)),
            dma((2,)),
            dma((2,)),
            dma((n_gy,)),
            dma((n_gy,)),
            dma((n_gy,)),
            dma((2,)),
            dma((n_gy,)),
            dma((2,)),
            dma((n_gy,)),
            dma((n_gy,)),
            dma((n_gy,)),
            dma((n_gy,)),
            dma((n_gy,)),
            dma((n_gy,)),
            dma((n_gx,)),
            dma((n_gx,)),
        ]
        warp, sent = pl.pallas_call(
            functools.partial(kernel, n_gx, n_gy, rows * 128 // devices),
            out_shape=(
                jax.ShapeDtypeStruct((rm, cm), F32),
                jax.ShapeDtypeStruct((n_gx, n_gy, 128), F32),
            ),
            in_specs=[hbm, hbm, smem, smem, smem, hbm, hbm, hbm, hbm],
            out_specs=(hbm, hbm),
            scratch_shapes=scratch,
            compiler_params=pltpu.CompilerParams(
                collective_id=0, has_side_effects=True, vmem_limit_bytes=56 * 2**20
            ),
        )(
            temp_start,
            heat_input,
            lateral,
            vertical,
            weighting,
            modulus,
            warp_prev,
            joint_cell.reshape(1, jpd),
            joint_owner.reshape(1, jpd),
        )
        warp, strain, resist = pl.pallas_call(
            finish_kernel,
            out_shape=(
                jax.ShapeDtypeStruct((rm, cm), F32),
                jax.ShapeDtypeStruct((2, rows, 128), F32),
                jax.ShapeDtypeStruct((rows, 128), F32),
            ),
            in_specs=[hbm, vmem, vmem, vmem],
            out_specs=(hbm, vmem, vmem),
            scratch_shapes=[dma],
            compiler_params=pltpu.CompilerParams(vmem_limit_bytes=16 * 2**20),
        )(
            warp,
            sent.reshape(devices, 128),
            joint_strain.reshape(2, rows, 128),
            joint_resist.reshape(rows, 128),
        )
        return (
            warp,
            strain.reshape(joint_strain.shape),
            resist.reshape(joint_resist.shape),
        )

    return jax.shard_map(
        body,
        mesh=mesh,
        in_specs=(
            P(None, ("gx", "gy"), None),
            P(None, ("gx", "gy"), None),
            P(),
            P(),
            P(),
            P("gx", "gy"),
            P("gx", "gy"),
            P(("gx", "gy")),
            P(("gx", "gy"), None),
            P(None, ("gx", "gy"), None),
            P(("gx", "gy"), None),
        ),
        out_specs=(P("gx", "gy"), P(None, ("gx", "gy"), None), P(("gx", "gy"), None)),
        check_vma=False,
    )
```

```python
import functools

import jax
import jax.numpy as jnp
from jax import lax
from jax.experimental import pallas as pl
from jax.experimental.pallas import tpu as pltpu
from jax.sharding import PartitionSpec as P

MESH = pl.DeviceIdType.MESH
F32 = jnp.float32
BF16 = jnp.bfloat16

stiffness = 0.2
shear_mod = 0.6
rate_scale = 0.5
sat_level = 2.5
sat_power = 0.3
harden = 2.0
LN2 = 0.6931471805599453


def iota(shape, dim):
    return lax.broadcasted_iota(jnp.int32, shape, dim)


def split(x):
    hi = x.astype(BF16)
    return hi, (x - hi.astype(F32)).astype(BF16)


def layer_weights(lat, ver, w):
    n = len(w)

    def add(x, y):
        return y if x is None else x if y is None else x + y

    def mul(x, y):
        return None if x is None else x * y

    def vert(x):
        out = []
        for l in range(n):
            keep = 1.0
            if l < n - 1:
                keep = keep - ver[l]
            if l > 0:
                keep = keep - ver[l - 1]
            total = mul(x[l], keep)
            if l > 0:
                total = add(total, mul(x[l - 1], ver[l - 1]))
            if l < n - 1:
                total = add(total, mul(x[l + 1], ver[l]))
            out.append(total)
        return out

    u = vert(w)
    wd = [mul(x, d) for x, d in zip(w, lat)]
    a0 = vert(u)
    a1 = [add(mul(x, d), y) for x, d, y in zip(u, lat, vert(wd))]
    a2 = [mul(x, d) for x, d in zip(wd, lat)]
    b0 = [add(x, y) for x, y in zip(u, w)]
    return (a0, b0), (a1, wd), (a2, [None] * n)


def kernel(
    n_gx,
    n_gy,
    cap,
    temp_ref,
    heat_ref,
    lat_ref,
    ver_ref,
    wei_ref,
    mod_ref,
    prev_ref,
    cell_ref,
    owner_ref,
    warp_out,
    rows_out,
    tbuf,
    hbuf,
    sums,
    msg_s,
    msg_r,
    cross_s,
    cross_r,
    edge_s,
    edge_r,
    col_s,
    col_r,
    mw,
    wbuf,
    coef,
    load,
    f_hi,
    f_lo,
    oh_col,
    oh_own,
    slot_of,
    owner_of,
    cell_r,
    reply_s,
    reply_r,
    inc_of,
    theta_of,
    out_s,
    load_sem,
    mw_sem,
    aux_sem,
    out_sem,
    col_ss,
    col_rs,
    row_ss,
    row_rs,
    msg_ss,
    msg_rs,
    cross_ss,
    cross_rs,
    edge_ss,
    edge_rs,
    ask_ss,
    ask_rs,
    reply_ss,
    reply_rs,
    joint_ss,
    joint_rs,
):
    layers, tr, columns = temp_ref.shape
    rm, cm = mod_ref.shape
    blocks = tr // 8
    ext = cm + 128
    cj = cm // 128
    devices = n_gx * n_gy
    jpd = cell_ref.shape[1]
    gx, gy = lax.axis_index("gx"), lax.axis_index("gy")
    last_x, last_y = n_gx - 1, n_gy - 1
    base = 16
    below = base + rm

    def remote(src, dst, ss, rs, to):
        return pltpu.make_async_remote_copy(
            src_ref=src,
            dst_ref=dst,
            send_sem=ss,
            recv_sem=rs,
            device_id=to,
            device_id_type=MESH,
        )

    def chunk_of(k):
        return lax.rem(gy + k, n_gy)

    def chunk_copies(k):
        cols = pl.ds(pl.multiple_of(chunk_of(k) * cm, cm), cm)
        return (
            pltpu.make_async_copy(temp_ref.at[:, :, cols], tbuf.at[k], load_sem.at[0, k]),
            pltpu.make_async_copy(heat_ref.at[:, :, cols], hbuf.at[k], load_sem.at[1, k]),
        )

    def mw_copies():
        return [
            pltpu.make_async_copy(
                ref.at[:, pl.ds(j * 128, 128)],
                mw.at[i, j, pl.ds(base, rm), :],
                mw_sem.at[i, j],
            )
            for i, ref in enumerate((mod_ref, prev_ref))
            for j in range(cj)
        ]

    aux = (
        pltpu.make_async_copy(cell_ref, cell_r.at[gy], aux_sem.at[0]),
        pltpu.make_async_copy(owner_ref, owner_of, aux_sem.at[1]),
    )

    @pl.loop(0, 3)
    def _(k):
        for copy in chunk_copies(k):
            copy.start()

    for copy in mw_copies():
        copy.start()
    for copy in aux:
        copy.start()

    @pl.loop(3, n_gy)
    def _(k):
        for copy in chunk_copies(k):
            copy.start()

    @pl.when(gy == last_y)
    def _():
        col_r[0] = jnp.zeros_like(col_r[0])

    @pl.when(gy == 0)
    def _():
        col_r[1] = jnp.zeros_like(col_r[1])

    zero8 = jnp.zeros((8, 128), F32)

    @pl.when(gx == last_x)
    def _():
        for i in range(2):
            for j in range(cj + 1):
                mw[i, j, below : below + 8, :] = zero8
        cross_r[0] = jnp.zeros_like(cross_r[0])
        edge_r[0] = jnp.zeros_like(edge_r[0])

    @pl.when(gx == 0)
    def _():
        for i in range(2):
            for j in range(cj + 1):
                mw[i, j, base - 8 : base, :] = zero8
        cross_r[1] = jnp.zeros_like(cross_r[1])
        edge_r[1] = jnp.zeros_like(edge_r[1])

    barrier = pltpu.get_barrier_semaphore()

    def device(o):
        return (lax.div(o, n_gy), lax.rem(o, n_gy))

    def other(m):
        return lax.rem(gx * n_gy + gy + m, devices)

    @pl.loop(1, devices)
    def _(m):
        pl.semaphore_signal(
            barrier, inc=1, device_id=device(other(m)), device_id_type=MESH
        )

    lat = [lat_ref[i] for i in range(layers)]
    ver = [ver_ref[i] for i in range(layers - 1)]
    wei = [wei_ref[i] for i in range(layers)]
    fields = [
        layer_weights(lat, ver, wei),
        layer_weights(lat, ver, [None] * (layers - 1) + [1.0]),
    ]

    zero_cols = jnp.zeros((tr, 128), F32)
    for f in range(2):
        for p in range(3):
            sums[f, p, :, 0:128] = zero_cols
            sums[f, p, :, columns + 128 : columns + 256] = zero_cols
    for j in range(cj + 1):
        for rows in (slice(0, 8), slice(below + 8, below + 16)):
            for ref in (mw.at[0], mw.at[1], wbuf.at[0], wbuf.at[1]):
                ref[j, rows, :] = zero8

    def layer_sums(k):
        for copy in chunk_copies(k):
            copy.wait()
        start = 128 + chunk_of(k) * cm
        for j in range(cj):
            lanes = slice(j * 128, j * 128 + 128)
            acc = [[None] * 3, [None] * 3]
            for l in range(layers):
                t, h = tbuf[k, l, :, lanes], hbuf[k, l, :, lanes]
                for f in range(2):
                    for p in range(3):
                        a, b = fields[f][p]
                        for c, x in ((a[l], t), (b[l], h)):
                            if c is not None:
                                term = c * x
                                acc[f][p] = (
                                    term if acc[f][p] is None else acc[f][p] + term
                                )
            where = pl.ds(pl.multiple_of(start + j * 128, 128), 128)
            for f in range(2):
                for p in range(3):
                    sums[f, p, :, where] = acc[f][p]

    wide = cm + 256
    crow = tr + 8

    def neighbours(x):
        r, c = x.shape
        return (
            pltpu.roll(x, 1, 0)
            + pltpu.roll(x, r - 1, 0)
            + pltpu.roll(x, 1, 1)
            + pltpu.roll(x, c - 1, 1)
            - 4.0 * x
        )

    def contribution(f, c):
        window = pl.ds(pl.multiple_of(c * cm, cm), wide)
        zero = jnp.zeros((8, wide), F32)
        p0, p1, p2 = (
            jnp.concatenate([sums[f, p, :, window], zero], axis=0) for p in range(3)
        )
        q = p1 + neighbours(p2)
        col = c * cm - 128 + iota((crow, wide), 1)
        row = iota((crow, wide), 0)
        panel = (col >= 0) & (col < columns)
        panel = panel & ((row < tr + 4) | (gx > 0) | (gy > 0))
        panel = panel & (
            (row < tr) | (row >= tr + 4) | (gx < last_x) | (gy < last_y)
        )
        q = jnp.where(panel, q, 0.0)
        out = p0 + neighbours(q)
        main = out[:, 128 : 128 + cm]
        lane = iota((crow, 128), 1)
        halo = jnp.where(lane < 64, out[:, 128 + cm :], out[:, 0:128])
        return main, halo

    lane8 = iota((8, 128), 1)
    sub8 = iota((8, 128), 0)
    sub_h = iota((8, cm // 2), 0)
    sub_e = iota((8, ext), 0)
    half = cm // 2
    at = blocks * cm

    def write_message(ref, main, halo):
        for b in range(blocks):
            ref[:, b * cm : b * cm + cm] = main[8 * b : 8 * b + 8]
        edge = main[tr:]
        ref[:, at : at + half] = jnp.where(
            (sub_h < 2) | (sub_h >= 6), edge[:, :half], pltpu.roll(edge[:, half:], 4, 0)
        )
        packed = halo[0:8]
        for b in range(1, blocks + 1):
            here = (lane8 >= 8 * b - 2) & (lane8 < 8 * b + 2)
            packed = jnp.where(
                here, pltpu.roll(halo[8 * b : 8 * b + 8], 8 * b, 1), packed
            )
        ref[:, at + half : at + half + 128] = packed

    def msg_copy(k):
        return remote(
            msg_s.at[k], msg_r.at[gy], msg_ss.at[k], msg_rs.at[gy], (gx, chunk_of(k))
        )

    def msg_arrival(s):
        return remote(msg_s.at[0], msg_r.at[s], msg_ss.at[0], msg_rs.at[s], (gx, s))

    def beyond(side):
        return gx - 1 if side == 0 else gx + 1

    def cross_copy(side, k):
        return remote(
            cross_s.at[k],
            cross_r.at[side],
            cross_ss.at[k],
            cross_rs.at[side],
            (beyond(side), chunk_of(k)),
        )

    def edge_copy(side, k):
        return remote(
            edge_s.at[k],
            edge_r.at[side],
            edge_ss.at[k],
            edge_rs.at[side],
            (beyond(side), chunk_of(k)),
        )

    sends_up = (gy == 0) & (gx > 0)
    sends_down = (gy == last_y) & (gx < last_x)

    def prepare(k, to_ref):
        main, halo = contribution(0, chunk_of(k))
        write_message(to_ref, main, halo)

        @pl.when(sends_up)
        def _():
            block = jnp.concatenate([main, halo], axis=1)
            cross_s[k] = jnp.where(sub_e < 4, block[0:8], block[tr:])

        @pl.when(sends_down)
        def _():
            block = jnp.concatenate([main, halo], axis=1)
            cross_s[k] = jnp.where(sub_e >= 4, block[tr - 8 : tr], block[tr:])

    def send_cross(copy_of, k):
        @pl.when(sends_up)
        def _():
            copy_of(0, k).start()

        @pl.when(sends_down)
        def _():
            copy_of(1, k).start()

    layer_sums(0)
    layer_sums(1)
    layer_sums(2)
    prepare(1, msg_s.at[1])

    pl.semaphore_wait(barrier, devices - 1)

    msg_copy(1).start()
    send_cross(cross_copy, 1)

    def ask_copy(d):
        return remote(
            cell_ref, cell_r.at[gy], ask_ss.at[d], ask_rs.at[gy], (gx, chunk_of(d))
        )

    def ask_arrival(s):
        return remote(cell_ref, cell_r.at[s], ask_ss.at[0], ask_rs.at[s], (gx, s))

    for copy in mw_copies():
        copy.wait()
    for i in range(2):
        to_left, to_right = zero8, zero8
        for b in range(rm // 8):
            here = (lane8 >= 4 * b) & (lane8 < 4 * b + 4)
            rows = slice(base + 8 * b, base + 8 * b + 8)
            to_left = jnp.where(here, pltpu.roll(mw[i, 0, rows, :], 4 * b, 1), to_left)
            to_right = jnp.where(
                here,
                pltpu.roll(mw[i, cj - 1, rows, :], (4 * b + 4) % 128, 1),
                to_right,
            )
        col_s[0, i] = to_left
        col_s[1, i] = to_right

    def col_copy(side, to):
        return remote(
            col_s.at[side], col_r.at[side], col_ss.at[side], col_rs.at[side], (gx, to)
        )

    @pl.when(gy > 0)
    def _():
        col_copy(0, gy - 1).start()

    @pl.when(gy < last_y)
    def _():
        col_copy(1, gy + 1).start()

    @pl.loop(1, n_gy)
    def _(d):
        ask_copy(d).start()

    @pl.loop(3, n_gy + 1)
    def _(k):
        @pl.when(k < n_gy)
        def _():
            layer_sums(k)

        prepare(k - 1, msg_s.at[k - 1])
        msg_copy(k - 1).start()
        send_cross(cross_copy, k - 1)

    prepare(0, msg_r.at[gy])
    send_cross(cross_copy, 0)

    @pl.when(gy < last_y)
    def _():
        col_copy(0, gy).wait_recv()

    @pl.when(gy > 0)
    def _():
        col_copy(1, gy).wait_recv()

    for i in range(2):
        right, left = col_r[0, i], col_r[1, i]
        for b in range(rm // 8):
            mw[i, cj, base + 8 * b : base + 8 * b + 8, :] = jnp.where(
                lane8 < 64,
                pltpu.roll(right, (128 - 4 * b) % 128, 1),
                pltpu.roll(left, (256 - 4 * b - 4) % 128, 1),
            )

    def row_copy(side, to):
        src = base if side == 0 else below - 8
        dst = below if side == 0 else base - 8
        return remote(
            mw.at[:, :, pl.ds(src, 8), :],
            mw.at[:, :, pl.ds(dst, 8), :],
            row_ss.at[side],
            row_rs.at[side],
            (to, gy),
        )

    @pl.when(gx > 0)
    def _():
        row_copy(0, gx - 1).start()

    @pl.when(gx < last_x)
    def _():
        row_copy(1, gx + 1).start()

    for copy in aux:
        copy.wait()

    @pl.loop(1, n_gy)
    def _(d):
        ask_arrival(lax.rem(gy + d, n_gy)).wait_recv()

    jb = 256
    shift_c = cm.bit_length() - 1
    lane_rows = iota((128, jb), 0)

    def one_hot(rows, at_row):
        return (rows == at_row).astype(F32).astype(BF16)

    def select(table, row_of, cells_ref, to_ref):
        tall = table.shape[0]
        per = tall // cj
        lhs = jnp.concatenate(split(table), axis=1)
        ids = iota((tall, jb), 0)
        for i in range(jpd // jb):
            blk = slice(i * jb, i * jb + jb)
            cells = cells_ref[:, blk]
            row = row_of(lax.shift_right_logical(cells, shift_c))
            block = lax.shift_right_logical(cells & (cm - 1), 7)
            place = jnp.where(row >= 0, block * per + row, -1)
            oh = one_hot(lane_rows, cells & 127)
            got = jnp.dot(
                lhs, jnp.concatenate([oh, oh], axis=0), preferred_element_type=F32
            )
            to_ref[:, blk] = jnp.sum(
                jnp.where(ids == place, got, 0.0), axis=0, keepdims=True
            )

    def stacked(x):
        return jnp.concatenate([x[:, j * 128 : j * 128 + 128] for j in range(cj)], axis=0)

    def near_row(row):
        q = row - gy * tr
        inside = (q >= 0) & (q < tr + 2)
        before = (q < 0) & (q >= -2)
        return jnp.where(inside, q, jnp.where(before, q + crow, -1))

    def reply_copy(k):
        return remote(
            reply_s.at[k],
            reply_r.at[gy],
            reply_ss.at[k],
            reply_rs.at[gy],
            (gx, chunk_of(k)),
        )

    def reply_arrival(s):
        return remote(
            reply_s.at[0], reply_r.at[s], reply_ss.at[0], reply_rs.at[s], (gx, s)
        )

    def answer(k, to_ref):
        main, _halo = contribution(1, chunk_of(k))

        @pl.when(sends_up | sends_down)
        def _():
            edge_s[k] = main[tr:]

        send_cross(edge_copy, k)
        select(stacked(main), near_row, cell_r.at[chunk_of(k)], to_ref)

    @pl.loop(1, n_gy)
    def _(k):
        answer(k, reply_s.at[k])
        reply_copy(k).start()

    answer(0, reply_r.at[gy])

    step = 16
    lane_s = iota((step, 128), 1)

    def around(ref, start):
        rows = pl.ds(start, step)
        mid = [ref[j, rows, :] for j in range(cj + 1)]
        up = [ref[j, pl.ds(start - 1, step), :] for j in range(cj + 1)]
        down = [ref[j, pl.ds(start + 1, step), :] for j in range(cj + 1)]
        to_r = [pltpu.roll(x, 1, 1) for x in mid]
        to_l = [pltpu.roll(x, 127, 1) for x in mid]
        left = [jnp.where(lane_s == 0, to_r[j - 1], to_r[j]) for j in range(cj + 1)]
        right = [
            jnp.where(lane_s == 127, to_l[(j + 1) % (cj + 1)], to_l[j])
            for j in range(cj + 1)
        ]
        return mid, list(zip(up, down, left, right))

    @pl.when(gx < last_x)
    def _():
        row_copy(0, gx).wait_recv()

    @pl.when(gx > 0)
    def _():
        row_copy(1, gx).wait_recv()

    halo_ok = ((lane_s < 64) & (gy < last_y)) | ((lane_s >= 64) & (gy > 0))

    for i in range((rm + 16) // step):
        start = base - 8 + i * step
        rows = pl.ds(start, step)
        mid, near = around(mw.at[0], start)
        row = start + iota((step, 128), 0)
        ok = ((row >= base) | (gx > 0)) & ((row < below) | (gx < last_x))
        for j in range(cj + 1):
            faces = [0.5 * (mid[j] + x) for x in near[j]]
            denom = stiffness + faces[0] + faces[1] + faces[2] + faces[3]
            inv = jnp.where(ok & halo_ok if j == cj else ok, 1.0 / denom, 0.0)
            for n, face in enumerate(faces):
                coef[n, j, rows, :] = face * inv
            coef[4, j, rows, :] = inv

    upper = (iota((jb, jb), 0) < iota((jb, jb), 1)).astype(F32).astype(BF16)
    own_rows = iota((devices, jb), 0)
    col_rows = iota((cm, jb), 0)
    carry = jnp.zeros((devices, 1), F32)
    for i in range(jpd // jb):
        blk = slice(i * jb, i * jb + jb)
        oh_col[:, blk] = one_hot(col_rows, cell_r[gy, :, blk] & (cm - 1))
        owner = owner_of[:, blk]
        oh = (own_rows == owner).astype(F32)
        oh_own[:, blk] = oh.astype(BF16)
        before = jnp.dot(oh.astype(BF16), upper, preferred_element_type=F32)
        slot_of[:, blk] = jnp.sum(oh * (before + carry), axis=0, keepdims=True)
        carry = carry + jnp.sum(oh, axis=1, keepdims=True)

    for j in range(cj + 1):
        for rows in (slice(base - 8, base), slice(below, below + 8)):
            load[j, rows, :] = zero8

    @pl.loop(0, n_gy)
    def _(d):
        s = lax.rem(gy + n_gy - d, n_gy)

        @pl.when(d > 0)
        def _():
            msg_arrival(s).wait_recv()

        packed = msg_r[s, :, at + half : at + half + 128]
        for b in range(blocks):
            rows = pl.ds(pl.multiple_of(base + s * tr + 8 * b, 8), 8)
            for j in range(cj):
                lanes = slice(b * cm + j * 128, b * cm + j * 128 + 128)
                load[j, rows, :] = msg_r[s, :, lanes] * coef[4, j, rows, :]
            halo = packed if b == 0 else pltpu.roll(packed, 128 - 8 * b, 1)
            load[cj, rows, :] = halo * coef[4, cj, rows, :]

    def add_edges(start, keep, parts):
        rows = pl.ds(start, 8)
        for j, x in enumerate(parts):
            load[j, rows, :] = load[j, rows, :] + jnp.where(
                keep, x * coef[4, j, rows, :], 0.0
            )

    for s in range(n_gy):
        both = [msg_r[s, :, at + j * 128 : at + j * 128 + 128] for j in range(cj // 2)]
        parts = both + [pltpu.roll(x, 4, 0) for x in both]
        parts.append(
            pltpu.roll(msg_r[s, :, at + half : at + half + 128], 128 - 8 * blocks, 1)
        )
        add_edges(base + (s + 1) * tr, sub8 < 2, parts)
        add_edges(base + s * tr - 8, sub8 >= 6, parts)

    @pl.when(gx < last_x)
    def _():
        cross_copy(0, 0).wait_recv()
        parts = [cross_r[0, :, j * 128 : j * 128 + 128] for j in range(cj + 1)]
        add_edges(below, sub8 < 2, parts)
        add_edges(below - 8, sub8 >= 6, parts)

    @pl.when(gx > 0)
    def _():
        cross_copy(1, 0).wait_recv()
        parts = [cross_r[1, :, j * 128 : j * 128 + 128] for j in range(cj + 1)]
        add_edges(base, sub8 < 2, parts)
        add_edges(base - 8, sub8 >= 6, parts)

    def swept(start, j, near):
        rows = pl.ds(start, step)
        total = load[j, rows, :]
        for n, x in enumerate(near[j]):
            total = total + coef[n, j, rows, :] * x
        return total

    for src, dst in ((mw.at[1], wbuf.at[0]), (wbuf.at[0], wbuf.at[1])):
        for i in range((rm + 16) // step):
            start = base - 8 + i * step
            _mid, near = around(src, start)
            for j in range(cj + 1):
                dst[j, pl.ds(start, step), :] = swept(start, j, near)

    for i in range(rm // step):
        start = base + i * step
        rows = pl.ds(start, step)
        tile_rows = pl.ds(i * step, step)
        _mid, near = around(wbuf.at[1], start)
        for j in range(cj):
            lanes = slice(j * 128, j * 128 + 128)
            x = swept(start, j, near)
            wbuf[0, j, rows, :] = x
            hi, lo = split(x - mw[1, j, rows, :])
            f_hi[tile_rows, lanes] = hi
            f_lo[tile_rows, lanes] = lo

    results = [
        pltpu.make_async_copy(
            wbuf.at[0, j, pl.ds(base, rm), :],
            warp_out.at[:, pl.ds(j * 128, 128)],
            out_sem.at[j],
        )
        for j in range(cj)
    ]
    for copy in results:
        copy.start()

    tile_ids = iota((rm, jb), 0)
    for i in range(jpd // jb):
        blk = slice(i * jb, i * jb + jb)
        oh = oh_col[:, blk]
        got = jnp.dot(f_hi[...], oh, preferred_element_type=F32) + jnp.dot(
            f_lo[...], oh, preferred_element_type=F32
        )
        row = lax.shift_right_logical(cell_r[gy, :, blk], shift_c)
        inc_of[:, blk] = jnp.sum(
            jnp.where(tile_ids == row, got, 0.0), axis=0, keepdims=True
        )

    @pl.when(gx < last_x)
    def _():
        edge_copy(0, 0).wait_recv()

    @pl.when(gx > 0)
    def _():
        edge_copy(1, 0).wait_recv()

    def outer_row(row):
        return jnp.where(row < 2, row, jnp.where(row >= rm - 2, row - (rm - 8), -1))

    sub_c = iota((8, cm), 0)
    select(
        stacked(jnp.where(sub_c < 4, edge_r[1], edge_r[0])),
        outer_row,
        cell_r.at[gy],
        theta_of,
    )

    @pl.loop(1, n_gy)
    def _(d):
        reply_arrival(lax.rem(gy + d, n_gy)).wait_recv()

    theta = theta_of[...]
    for s in range(n_gy):
        theta = theta + reply_r[s]
    theta_of[...] = theta

    kk = iota((128, jb), 0)
    total = jnp.zeros((devices, 128), F32)
    for i in range(jpd // jb):
        blk = slice(i * jb, i * jb + jb)
        rank = slot_of[:, blk].astype(jnp.int32)
        value = jnp.where(kk < cap, inc_of[:, blk], theta_of[:, blk])
        here = (kk == rank) | (kk == rank + cap)
        value = jnp.where(here, value, (kk == 2 * cap).astype(F32))
        hi, lo = split(value)
        oh = oh_own[:, blk]
        for part in (hi, lo):
            total = total + lax.dot_general(
                oh, part, (((1,), (1,)), ((), ())), preferred_element_type=F32
            )
    for o in range(devices):
        out_s[o] = total[o : o + 1]

    me = gx * n_gy + gy

    def joint_copy(m):
        o = other(m)
        return remote(out_s.at[o], rows_out.at[me], joint_ss, joint_rs, device(o))

    @pl.loop(1, devices)
    def _(m):
        joint_copy(m).start()

    own = pltpu.make_async_copy(out_s.at[me], rows_out.at[me], aux_sem.at[2])
    own.start()

    for copy in results:
        copy.wait()

    @pl.when(gy > 0)
    def _():
        col_copy(0, gy - 1).wait_send()

    @pl.when(gy < last_y)
    def _():
        col_copy(1, gy + 1).wait_send()

    @pl.when(gx > 0)
    def _():
        row_copy(0, gx - 1).wait_send()

    @pl.when(gx < last_x)
    def _():
        row_copy(1, gx + 1).wait_send()

    @pl.loop(1, n_gy)
    def _(k):
        msg_copy(k).wait_send()
        ask_copy(k).wait_send()
        reply_copy(k).wait_send()

    for side, sends in ((0, sends_up), (1, sends_down)):

        @pl.when(sends)
        def _():
            @pl.loop(0, n_gy)
            def _(k):
                cross_copy(side, k).wait_send()
                edge_copy(side, k).wait_send()

    own.wait()
    every = pl.ds(0, devices - 1)
    all_joints = remote(
        out_s.at[every], rows_out.at[every], joint_ss, joint_rs, (gx, gy)
    )
    all_joints.wait_send()
    all_joints.wait_recv()


def finish_kernel(
    warp_hbm,
    rows_hbm,
    strain_hbm,
    resist_hbm,
    warp_out,
    strain_out,
    resist_out,
    rows_ref,
    strain_ref,
    resist_ref,
    held,
    sem,
):
    loads = [
        pltpu.make_async_copy(src, dst, sem.at[i])
        for i, (src, dst) in enumerate(
            (
                (rows_hbm, rows_ref),
                (strain_hbm, strain_ref),
                (resist_hbm, resist_ref),
            )
        )
    ]
    for load in loads:
        load.start()
    parts_of_warp = 4
    share = warp_hbm.shape[0] // parts_of_warp
    warp_rows = [pl.ds(n * share, share) for n in range(parts_of_warp)]
    into = [
        pltpu.make_async_copy(warp_hbm.at[r], held.at[r], sem.at[3 + n])
        for n, r in enumerate(warp_rows)
    ]
    out = [
        pltpu.make_async_copy(held.at[r], warp_out.at[r], sem.at[3 + n])
        for n, r in enumerate(warp_rows)
    ]
    for copy in into:
        copy.start()
    for first, then in zip(into, out):
        first.wait()
        then.start()
    for load in loads:
        load.wait()
    devices = rows_ref.shape[0]
    cap = resist_ref.shape[0] * 128 // devices
    groups = devices // 8
    per = 8 * cap // 128
    parts = [rows_ref[pl.ds(i, groups, stride=8), :] for i in range(8)]
    counts = [jnp.broadcast_to(p[:, 2 * cap : 2 * cap + 1], (groups, 128)) for p in parts]
    lane = iota((groups, 128), 1)
    for m in range(per):
        inc = theta = jnp.zeros((groups, 128), F32)
        live = jnp.zeros((groups, 128), F32)
        for i in range(8):
            lo, hi = max(i * cap, m * 128), min((i + 1) * cap, m * 128 + 128)
            if lo >= hi:
                continue
            here = (lane >= lo - m * 128) & (lane < hi - m * 128)
            shift = (i * cap - m * 128) % 128
            inc = jnp.where(here, pltpu.roll(parts[i], shift, 1), inc)
            theta = jnp.where(here, pltpu.roll(parts[i], (shift - cap) % 128, 1), theta)
            slot = (lane + (m * 128 - i * cap)).astype(F32)
            live = jnp.where(here, jnp.where(slot < counts[i], 1.0, 0.0), live)
        rows = pl.ds(m, groups, stride=per)
        total0, inelastic, resist = (
            strain_ref[0, rows, :],
            strain_ref[1, rows, :],
            resist_ref[rows, :],
        )
        total_new = total0 + inc
        arrhen = jnp.exp(2.0 - 2.0 / (1.0 + 0.1 * theta * theta))
        arg = shear_mod * (total_new - inelastic) / resist
        hyper = jnp.exp(arg - LN2) - jnp.exp(-arg - LN2)
        rate = rate_scale * arrhen * hyper * jnp.abs(hyper)
        size = jnp.abs(rate)
        target = sat_level * jnp.exp(sat_power * jnp.log(1.0 + size / arrhen))
        resist_new = resist + harden * (1.0 - resist / target) * size
        keep = live > 0.5
        strain_out[0, rows, :] = jnp.where(keep, total_new, total0)
        strain_out[1, rows, :] = jnp.where(keep, inelastic + rate, inelastic)
        resist_out[rows, :] = jnp.where(keep, resist_new, resist)
    for copy in out:
        copy.wait()


def solution(mesh):
    n_gx, n_gy = mesh.shape["gx"], mesh.shape["gy"]
    devices = n_gx * n_gy

    def body(
        temp_start,
        heat_input,
        lateral,
        vertical,
        weighting,
        modulus,
        warp_prev,
        joint_cell,
        joint_owner,
        joint_strain,
        joint_resist,
    ):
        layers, tr, columns = temp_start.shape
        rm, cm = modulus.shape
        jpd = joint_cell.shape[0]
        rows = joint_resist.shape[1] // 128
        blocks = tr // 8
        mwide = blocks * cm + cm // 2 + 128
        ext, cb, tall = cm + 128, cm // 128 + 1, rm + 32
        hbm = pl.BlockSpec(memory_space=pl.ANY)
        smem = pl.BlockSpec(memory_space=pltpu.SMEM)
        vmem = pl.BlockSpec(memory_space=pltpu.VMEM)
        dma = pltpu.SemaphoreType.DMA
        scratch = [
            pltpu.VMEM((n_gy, layers, tr, cm), F32),
            pltpu.VMEM((n_gy, layers, tr, cm), F32),
            pltpu.VMEM((2, 3, tr, columns + 256), F32),
            pltpu.VMEM((n_gy, 8, mwide), F32),
            pltpu.VMEM((n_gy, 8, mwide), F32),
            pltpu.VMEM((n_gy, 8, ext), F32),
            pltpu.VMEM((2, 8, ext), F32),
            pltpu.VMEM((n_gy, 8, cm), F32),
            pltpu.VMEM((2, 8, cm), F32),
            pltpu.VMEM((2, 2, 8, 128), F32),
            pltpu.VMEM((2, 2, 8, 128), F32),
            pltpu.VMEM((2, cb, tall, 128), F32),
            pltpu.VMEM((2, cb, tall, 128), F32),
            pltpu.VMEM((5, cb, tall, 128), F32),
            pltpu.VMEM((cb, tall, 128), F32),
            pltpu.VMEM((rm, cm), BF16),
            pltpu.VMEM((rm, cm), BF16),
            pltpu.VMEM((cm, jpd), BF16),
            pltpu.VMEM((devices, jpd), BF16),
            pltpu.VMEM((1, jpd), F32),
            pltpu.VMEM((1, jpd), jnp.int32),
            pltpu.VMEM((n_gy, 1, jpd), jnp.int32),
            pltpu.VMEM((n_gy, 1, jpd), F32),
            pltpu.VMEM((n_gy, 1, jpd), F32),
            pltpu.VMEM((1, jpd), F32),
            pltpu.VMEM((1, jpd), F32),
            pltpu.VMEM((devices, 1, 128), F32),
            dma((2, n_gy)),
            dma((2, cb - 1)),
            dma((3,)),
            dma((cb - 1,)),
            dma((2,)),
            dma((2,)),
            dma((2,)),
            dma((2,)),
            dma((n_gy,)),
            dma((n_gy,)),
            dma((n_gy,)),
            dma((2,)),
            dma((n_gy,)),
            dma((2,)),
            dma((n_gy,)),
            dma((n_gy,)),
            dma((n_gy,)),
            dma((n_gy,)),
            dma,
            dma,
        ]
        warp, sent = pl.pallas_call(
            functools.partial(kernel, n_gx, n_gy, rows * 128 // devices),
            out_shape=(
                jax.ShapeDtypeStruct((rm, cm), F32),
                jax.ShapeDtypeStruct((devices, 1, 128), F32),
            ),
            in_specs=[hbm, hbm, smem, smem, smem, hbm, hbm, hbm, hbm],
            out_specs=(hbm, hbm),
            scratch_shapes=scratch,
            compiler_params=pltpu.CompilerParams(
                collective_id=0, has_side_effects=True, vmem_limit_bytes=56 * 2**20
            ),
        )(
            temp_start,
            heat_input,
            lateral,
            vertical,
            weighting,
            modulus,
            warp_prev,
            joint_cell.reshape(1, jpd),
            joint_owner.reshape(1, jpd),
        )
        warp, strain, resist = pl.pallas_call(
            finish_kernel,
            out_shape=(
                jax.ShapeDtypeStruct((rm, cm), F32),
                jax.ShapeDtypeStruct((2, rows, 128), F32),
                jax.ShapeDtypeStruct((rows, 128), F32),
            ),
            in_specs=[hbm, hbm, hbm, hbm],
            out_specs=(hbm, vmem, vmem),
            scratch_shapes=[
                pltpu.VMEM((devices, 128), F32),
                pltpu.VMEM((2, rows, 128), F32),
                pltpu.VMEM((rows, 128), F32),
                pltpu.VMEM((rm, cm), F32),
                dma((7,)),
            ],
            compiler_params=pltpu.CompilerParams(vmem_limit_bytes=60 * 2**20),
        )(
            warp,
            sent.reshape(devices, 128),
            joint_strain.reshape(2, rows, 128),
            joint_resist.reshape(rows, 128),
        )
        return (
            warp,
            strain.reshape(joint_strain.shape),
            resist.reshape(joint_resist.shape),
        )

    return jax.shard_map(
        body,
        mesh=mesh,
        in_specs=(
            P(None, ("gx", "gy"), None),
            P(None, ("gx", "gy"), None),
            P(),
            P(),
            P(),
            P("gx", "gy"),
            P("gx", "gy"),
            P(("gx", "gy")),
            P(("gx", "gy"), None),
            P(None, ("gx", "gy"), None),
            P(("gx", "gy"), None),
        ),
        out_specs=(P("gx", "gy"), P(None, ("gx", "gy"), None), P(("gx", "gy"), None)),
        check_vma=False,
    )
```

```python
import functools

import jax
import jax.numpy as jnp
from jax import lax
from jax.experimental import pallas as pl
from jax.experimental.pallas import tpu as pltpu
from jax.sharding import PartitionSpec as P

MESH = pl.DeviceIdType.MESH
F32 = jnp.float32
BF16 = jnp.bfloat16

stiffness = 0.2
shear_mod = 0.6
rate_scale = 0.5
sat_level = 2.5
sat_power = 0.3
harden = 2.0
LN2 = 0.6931471805599453


def iota(shape, dim):
    return lax.broadcasted_iota(jnp.int32, shape, dim)


def split(x):
    hi = x.astype(BF16)
    return hi, (x - hi.astype(F32)).astype(BF16)


def layer_weights(lat, ver, w):
    n = len(w)

    def add(x, y):
        return y if x is None else x if y is None else x + y

    def mul(x, y):
        return None if x is None else x * y

    def vert(x):
        out = []
        for l in range(n):
            keep = 1.0
            if l < n - 1:
                keep = keep - ver[l]
            if l > 0:
                keep = keep - ver[l - 1]
            total = mul(x[l], keep)
            if l > 0:
                total = add(total, mul(x[l - 1], ver[l - 1]))
            if l < n - 1:
                total = add(total, mul(x[l + 1], ver[l]))
            out.append(total)
        return out

    u = vert(w)
    wd = [mul(x, d) for x, d in zip(w, lat)]
    a0 = vert(u)
    a1 = [add(mul(x, d), y) for x, d, y in zip(u, lat, vert(wd))]
    a2 = [mul(x, d) for x, d in zip(wd, lat)]
    b0 = [add(x, y) for x, y in zip(u, w)]
    return (a0, b0), (a1, wd), (a2, [None] * n)


def kernel(
    n_gx,
    n_gy,
    cap,
    temp_ref,
    heat_ref,
    lat_ref,
    ver_ref,
    wei_ref,
    mod_ref,
    prev_ref,
    cell_ref,
    owner_ref,
    warp_out,
    rows_out,
    tbuf,
    hbuf,
    sums,
    msg_s,
    msg_r,
    cross_s,
    cross_r,
    edge_s,
    edge_r,
    col_s,
    col_r,
    mw,
    wbuf,
    coef,
    load,
    f_parts,
    oh_col,
    oh_own,
    slot_of,
    owner_of,
    cell_r,
    reply_s,
    reply_r,
    inc_of,
    theta_of,
    out_s,
    load_sem,
    mw_sem,
    aux_sem,
    out_sem,
    col_ss,
    col_rs,
    row_ss,
    row_rs,
    msg_ss,
    msg_rs,
    cross_ss,
    cross_rs,
    edge_ss,
    edge_rs,
    ask_ss,
    ask_rs,
    reply_ss,
    reply_rs,
    joint_ss,
    joint_rs,
):
    layers, tr, columns = temp_ref.shape
    rm, cm = mod_ref.shape
    blocks = tr // 8
    ext = cm + 128
    cj = cm // 128
    devices = n_gx * n_gy
    jpd = cell_ref.shape[1]
    gx, gy = lax.axis_index("gx"), lax.axis_index("gy")
    last_x, last_y = n_gx - 1, n_gy - 1
    base = 16
    below = base + rm

    def remote(src, dst, ss, rs, to):
        return pltpu.make_async_remote_copy(
            src_ref=src,
            dst_ref=dst,
            send_sem=ss,
            recv_sem=rs,
            device_id=to,
            device_id_type=MESH,
        )

    def chunk_of(k):
        return lax.rem(gy + k, n_gy)

    def chunk_copies(k):
        cols = pl.ds(pl.multiple_of(chunk_of(k) * cm, cm), cm)
        return (
            pltpu.make_async_copy(temp_ref.at[:, :, cols], tbuf.at[k], load_sem.at[0, k]),
            pltpu.make_async_copy(heat_ref.at[:, :, cols], hbuf.at[k], load_sem.at[1, k]),
        )

    def mw_copies():
        return [
            pltpu.make_async_copy(
                ref.at[:, pl.ds(j * 128, 128)],
                mw.at[i, j, pl.ds(base, rm), :],
                mw_sem.at[i, j],
            )
            for i, ref in enumerate((mod_ref, prev_ref))
            for j in range(cj)
        ]

    aux = (
        pltpu.make_async_copy(cell_ref, cell_r.at[gy], aux_sem.at[0]),
        pltpu.make_async_copy(owner_ref, owner_of, aux_sem.at[1]),
    )

    @pl.loop(0, 3)
    def _(k):
        for copy in chunk_copies(k):
            copy.start()

    for copy in mw_copies():
        copy.start()
    for copy in aux:
        copy.start()

    @pl.loop(3, n_gy)
    def _(k):
        for copy in chunk_copies(k):
            copy.start()

    @pl.when(gy == last_y)
    def _():
        col_r[0] = jnp.zeros_like(col_r[0])

    @pl.when(gy == 0)
    def _():
        col_r[1] = jnp.zeros_like(col_r[1])

    zero8 = jnp.zeros((8, 128), F32)

    @pl.when(gx == last_x)
    def _():
        for i in range(2):
            for j in range(cj + 1):
                mw[i, j, below : below + 8, :] = zero8
        cross_r[0] = jnp.zeros_like(cross_r[0])
        edge_r[0] = jnp.zeros_like(edge_r[0])

    @pl.when(gx == 0)
    def _():
        for i in range(2):
            for j in range(cj + 1):
                mw[i, j, base - 8 : base, :] = zero8
        cross_r[1] = jnp.zeros_like(cross_r[1])
        edge_r[1] = jnp.zeros_like(edge_r[1])

    barrier = pltpu.get_barrier_semaphore()

    def wrapped(i, n):
        return jnp.where(i >= n, i - n, i)

    def for_others(act):
        for dy in range(1, n_gy):
            act((gx, wrapped(gy + dy, n_gy)))

        @pl.loop(1, n_gx)
        def _(dx):
            x = wrapped(gx + dx, n_gx)
            for dy in range(n_gy):
                act((x, wrapped(gy + dy, n_gy)))

    def greet(to):
        pl.semaphore_signal(barrier, inc=1, device_id=to, device_id_type=MESH)

    for_others(greet)

    lat = [lat_ref[i] for i in range(layers)]
    ver = [ver_ref[i] for i in range(layers - 1)]
    wei = [wei_ref[i] for i in range(layers)]
    fields = [
        layer_weights(lat, ver, wei),
        layer_weights(lat, ver, [None] * (layers - 1) + [1.0]),
    ]

    zero_cols = jnp.zeros((tr, 128), F32)
    for f in range(2):
        for p in range(3):
            sums[f, p, :, 0:128] = zero_cols
            sums[f, p, :, columns + 128 : columns + 256] = zero_cols
    for j in range(cj + 1):
        for rows in (slice(0, 8), slice(below + 8, below + 16)):
            for ref in (mw.at[0], mw.at[1], wbuf.at[0], wbuf.at[1]):
                ref[j, rows, :] = zero8

    def await_chunk(k):
        for copy in chunk_copies(k):
            copy.wait()

    def layer_sums(k):
        start = 128 + chunk_of(k) * cm
        for j in range(cj):
            lanes = slice(j * 128, j * 128 + 128)
            acc = [[None] * 3, [None] * 3]
            for l in range(layers):
                t, h = tbuf[k, l, :, lanes], hbuf[k, l, :, lanes]
                for f in range(2):
                    for p in range(3):
                        a, b = fields[f][p]
                        for c, x in ((a[l], t), (b[l], h)):
                            if c is not None:
                                term = c * x
                                acc[f][p] = (
                                    term if acc[f][p] is None else acc[f][p] + term
                                )
            where = pl.ds(pl.multiple_of(start + j * 128, 128), 128)
            for f in range(2):
                for p in range(3):
                    sums[f, p, :, where] = acc[f][p]

    wide = cm + 256
    crow = tr + 8

    def neighbours(x):
        r, c = x.shape
        return (
            pltpu.roll(x, 1, 0)
            + pltpu.roll(x, r - 1, 0)
            + pltpu.roll(x, 1, 1)
            + pltpu.roll(x, c - 1, 1)
            - 4.0 * x
        )

    def contribution(f, c):
        window = pl.ds(pl.multiple_of(c * cm, cm), wide)
        zero = jnp.zeros((8, wide), F32)
        p0, p1, p2 = (
            jnp.concatenate([sums[f, p, :, window], zero], axis=0) for p in range(3)
        )
        q = p1 + neighbours(p2)
        col = c * cm - 128 + iota((crow, wide), 1)
        row = iota((crow, wide), 0)
        panel = (col >= 0) & (col < columns)
        panel = panel & ((row < tr + 4) | (gx > 0) | (gy > 0))
        panel = panel & (
            (row < tr) | (row >= tr + 4) | (gx < last_x) | (gy < last_y)
        )
        q = jnp.where(panel, q, 0.0)
        out = p0 + neighbours(q)
        main = out[:, 128 : 128 + cm]
        lane = iota((crow, 128), 1)
        halo = jnp.where(lane < 64, out[:, 128 + cm :], out[:, 0:128])
        return main, halo

    lane8 = iota((8, 128), 1)
    sub8 = iota((8, 128), 0)
    sub_h = iota((8, cm // 2), 0)
    sub_e = iota((8, ext), 0)
    half = cm // 2
    at = blocks * cm

    def write_message(ref, main, halo):
        for b in range(blocks):
            ref[:, b * cm : b * cm + cm] = main[8 * b : 8 * b + 8]
        edge = main[tr:]
        ref[:, at : at + half] = jnp.where(
            (sub_h < 2) | (sub_h >= 6), edge[:, :half], pltpu.roll(edge[:, half:], 4, 0)
        )
        packed = halo[0:8]
        for b in range(1, blocks + 1):
            here = (lane8 >= 8 * b - 2) & (lane8 < 8 * b + 2)
            packed = jnp.where(
                here, pltpu.roll(halo[8 * b : 8 * b + 8], 8 * b, 1), packed
            )
        ref[:, at + half : at + half + 128] = packed

    def msg_copy(k):
        return remote(
            msg_s.at[k], msg_r.at[gy], msg_ss.at[k], msg_rs.at[gy], (gx, chunk_of(k))
        )

    def msg_arrival(s):
        return remote(msg_s.at[0], msg_r.at[s], msg_ss.at[0], msg_rs.at[s], (gx, s))

    def beyond(side):
        return gx - 1 if side == 0 else gx + 1

    def cross_copy(side, k):
        return remote(
            cross_s.at[k],
            cross_r.at[side],
            cross_ss.at[k],
            cross_rs.at[side],
            (beyond(side), chunk_of(k)),
        )

    def edge_copy(side, k):
        return remote(
            edge_s.at[k],
            edge_r.at[side],
            edge_ss.at[k],
            edge_rs.at[side],
            (beyond(side), chunk_of(k)),
        )

    sends_up = (gy == 0) & (gx > 0)
    sends_down = (gy == last_y) & (gx < last_x)

    def prepare(k, to_ref):
        main, halo = contribution(0, chunk_of(k))
        write_message(to_ref, main, halo)

        block = jnp.concatenate([main, halo], axis=1)
        inner = jnp.where(gy == 0, block[0:8], block[tr - 8 : tr])
        cross_s[k] = jnp.where((sub_e < 4) == (gy == 0), inner, block[tr:])

    def send_cross(copy_of, k):
        @pl.when(sends_up)
        def _():
            copy_of(0, k).start()

        @pl.when(sends_down)
        def _():
            copy_of(1, k).start()

    for k in range(3):
        await_chunk(k)
        layer_sums(k)
    prepare(1, msg_s.at[1])

    pl.semaphore_wait(barrier, devices - 1)

    msg_copy(1).start()
    send_cross(cross_copy, 1)

    def ask_copy(d):
        return remote(
            cell_ref, cell_r.at[gy], ask_ss.at[d], ask_rs.at[gy], (gx, chunk_of(d))
        )

    def ask_arrival(s):
        return remote(cell_ref, cell_r.at[s], ask_ss.at[0], ask_rs.at[s], (gx, s))

    for copy in mw_copies():
        copy.wait()
    for i in range(2):
        to_left, to_right = zero8, zero8
        for b in range(rm // 8):
            here = (lane8 >= 4 * b) & (lane8 < 4 * b + 4)
            rows = slice(base + 8 * b, base + 8 * b + 8)
            to_left = jnp.where(here, pltpu.roll(mw[i, 0, rows, :], 4 * b, 1), to_left)
            to_right = jnp.where(
                here,
                pltpu.roll(mw[i, cj - 1, rows, :], (4 * b + 4) % 128, 1),
                to_right,
            )
        col_s[0, i] = to_left
        col_s[1, i] = to_right

    def col_copy(side, to):
        return remote(
            col_s.at[side], col_r.at[side], col_ss.at[side], col_rs.at[side], (gx, to)
        )

    @pl.when(gy > 0)
    def _():
        col_copy(0, gy - 1).start()

    @pl.when(gy < last_y)
    def _():
        col_copy(1, gy + 1).start()

    @pl.loop(1, n_gy)
    def _(d):
        ask_copy(d).start()

    def send_load(k):
        msg_copy(k).start()
        send_cross(cross_copy, k)

    pairs = (n_gy - 4) // 2

    @pl.loop(0, pairs)
    def _(i):
        ks = (2 * i + 3, 2 * i + 4)
        for k in ks:
            await_chunk(k)
        for k in ks:
            layer_sums(k)
            prepare(k - 1, msg_s.at[k - 1])
        for k in ks:
            send_load(k - 1)

    for k in range(2 * pairs + 3, n_gy):
        await_chunk(k)
        layer_sums(k)
        prepare(k - 1, msg_s.at[k - 1])
        send_load(k - 1)
    prepare(n_gy - 1, msg_s.at[n_gy - 1])
    send_load(n_gy - 1)
    prepare(0, msg_r.at[gy])
    send_cross(cross_copy, 0)

    @pl.when(gy < last_y)
    def _():
        col_copy(0, gy).wait_recv()

    @pl.when(gy > 0)
    def _():
        col_copy(1, gy).wait_recv()

    for i in range(2):
        right, left = col_r[0, i], col_r[1, i]
        for b in range(rm // 8):
            mw[i, cj, base + 8 * b : base + 8 * b + 8, :] = jnp.where(
                lane8 < 64,
                pltpu.roll(right, (128 - 4 * b) % 128, 1),
                pltpu.roll(left, (256 - 4 * b - 4) % 128, 1),
            )

    def row_copy(side, to):
        src = base if side == 0 else below - 8
        dst = below if side == 0 else base - 8
        return remote(
            mw.at[:, :, pl.ds(src, 8), :],
            mw.at[:, :, pl.ds(dst, 8), :],
            row_ss.at[side],
            row_rs.at[side],
            (to, gy),
        )

    @pl.when(gx > 0)
    def _():
        row_copy(0, gx - 1).start()

    @pl.when(gx < last_x)
    def _():
        row_copy(1, gx + 1).start()

    for copy in aux:
        copy.wait()

    @pl.loop(1, n_gy)
    def _(d):
        ask_arrival(lax.rem(gy + d, n_gy)).wait_recv()

    jb = 256
    shift_c = cm.bit_length() - 1
    lane_rows = iota((128, jb), 0)

    def one_hot(rows, at_row):
        return (rows == at_row).astype(F32).astype(BF16)

    def select(table, row_of, cells_ref, to_ref):
        tall = table.shape[0]
        per = tall // cj
        lhs = jnp.concatenate(split(table), axis=1)
        ids = iota((tall, jb), 0)
        for i in range(jpd // jb):
            blk = slice(i * jb, i * jb + jb)
            cells = cells_ref[:, blk]
            row = row_of(lax.shift_right_logical(cells, shift_c))
            block = lax.shift_right_logical(cells & (cm - 1), 7)
            place = jnp.where(row >= 0, block * per + row, -1)
            oh = one_hot(lane_rows, cells & 127)
            got = jnp.dot(
                lhs, jnp.concatenate([oh, oh], axis=0), preferred_element_type=F32
            )
            to_ref[:, blk] = jnp.sum(
                jnp.where(ids == place, got, 0.0), axis=0, keepdims=True
            )

    def stacked(x):
        return jnp.concatenate([x[:, j * 128 : j * 128 + 128] for j in range(cj)], axis=0)

    def near_row(row):
        q = row - gy * tr
        inside = (q >= 0) & (q < tr + 2)
        before = (q < 0) & (q >= -2)
        return jnp.where(inside, q, jnp.where(before, q + crow, -1))

    def reply_copy(k):
        return remote(
            reply_s.at[k],
            reply_r.at[gy],
            reply_ss.at[k],
            reply_rs.at[gy],
            (gx, chunk_of(k)),
        )

    def reply_arrival(s):
        return remote(
            reply_s.at[0], reply_r.at[s], reply_ss.at[0], reply_rs.at[s], (gx, s)
        )

    group = 4

    @pl.loop(0, n_gy // group)
    def _(i):
        ks = [lax.rem(group * i + u + 1, n_gy) for u in range(group)]
        for k in ks:
            main, _halo = contribution(1, chunk_of(k))
            edge_s[k] = main[tr:]
            select(stacked(main), near_row, cell_r.at[chunk_of(k)], reply_s.at[k])
        for k in ks:
            send_cross(edge_copy, k)

            @pl.when(k > 0)
            def _():
                reply_copy(k).start()

    reply_r[gy] = reply_s[0]

    step = 16
    lane_s = iota((step, 128), 1)

    def around(ref, start):
        rows = pl.ds(start, step)
        mid = [ref[j, rows, :] for j in range(cj + 1)]
        up = [ref[j, pl.ds(start - 1, step), :] for j in range(cj + 1)]
        down = [ref[j, pl.ds(start + 1, step), :] for j in range(cj + 1)]
        to_r = [pltpu.roll(x, 1, 1) for x in mid]
        to_l = [pltpu.roll(x, 127, 1) for x in mid]
        left = [jnp.where(lane_s == 0, to_r[j - 1], to_r[j]) for j in range(cj + 1)]
        right = [
            jnp.where(lane_s == 127, to_l[(j + 1) % (cj + 1)], to_l[j])
            for j in range(cj + 1)
        ]
        return mid, list(zip(up, down, left, right))

    @pl.when(gx < last_x)
    def _():
        row_copy(0, gx).wait_recv()

    @pl.when(gx > 0)
    def _():
        row_copy(1, gx).wait_recv()

    halo_ok = ((lane_s < 64) & (gy < last_y)) | ((lane_s >= 64) & (gy > 0))

    for i in range((rm + 16) // step):
        start = base - 8 + i * step
        rows = pl.ds(start, step)
        mid, near = around(mw.at[0], start)
        row = start + iota((step, 128), 0)
        ok = ((row >= base) | (gx > 0)) & ((row < below) | (gx < last_x))
        for j in range(cj + 1):
            faces = [0.5 * (mid[j] + x) for x in near[j]]
            denom = stiffness + faces[0] + faces[1] + faces[2] + faces[3]
            inv = jnp.where(ok & halo_ok if j == cj else ok, 1.0 / denom, 0.0)
            for n, face in enumerate(faces):
                coef[n, j, rows, :] = face * inv
            coef[4, j, rows, :] = inv

    upper = (iota((jb, jb), 0) < iota((jb, jb), 1)).astype(F32).astype(BF16)
    own_rows = iota((devices, jb), 0)
    col_rows = iota((cm, jb), 0)
    carry = jnp.zeros((devices, 1), F32)
    for i in range(jpd // jb):
        blk = slice(i * jb, i * jb + jb)
        oh_col[:, blk] = one_hot(col_rows, cell_r[gy, :, blk] & (cm - 1))
        owner = owner_of[:, blk]
        oh = (own_rows == owner).astype(F32)
        oh_own[:, blk] = oh.astype(BF16)
        before = jnp.dot(oh.astype(BF16), upper, preferred_element_type=F32)
        slot_of[:, blk] = jnp.sum(oh * (before + carry), axis=0, keepdims=True)
        carry = carry + jnp.sum(oh, axis=1, keepdims=True)

    for j in range(cj + 1):
        for rows in (slice(base - 8, base), slice(below, below + 8)):
            load[j, rows, :] = zero8

    @pl.loop(0, n_gy)
    def _(d):
        s = lax.rem(gy + n_gy - d, n_gy)

        @pl.when(d > 0)
        def _():
            msg_arrival(s).wait_recv()

        packed = msg_r[s, :, at + half : at + half + 128]
        for b in range(blocks):
            rows = pl.ds(pl.multiple_of(base + s * tr + 8 * b, 8), 8)
            for j in range(cj):
                lanes = slice(b * cm + j * 128, b * cm + j * 128 + 128)
                load[j, rows, :] = msg_r[s, :, lanes] * coef[4, j, rows, :]
            halo = packed if b == 0 else pltpu.roll(packed, 128 - 8 * b, 1)
            load[cj, rows, :] = halo * coef[4, cj, rows, :]

    def add_edges(start, keep, parts):
        rows = pl.ds(start, 8)
        for j, x in enumerate(parts):
            load[j, rows, :] = load[j, rows, :] + jnp.where(
                keep, x * coef[4, j, rows, :], 0.0
            )

    for s in range(n_gy):
        both = [msg_r[s, :, at + j * 128 : at + j * 128 + 128] for j in range(cj // 2)]
        parts = both + [pltpu.roll(x, 4, 0) for x in both]
        parts.append(
            pltpu.roll(msg_r[s, :, at + half : at + half + 128], 128 - 8 * blocks, 1)
        )
        add_edges(base + (s + 1) * tr, sub8 < 2, parts)
        add_edges(base + s * tr - 8, sub8 >= 6, parts)

    @pl.when(gx < last_x)
    def _():
        cross_copy(0, 0).wait_recv()
        parts = [cross_r[0, :, j * 128 : j * 128 + 128] for j in range(cj + 1)]
        add_edges(below, sub8 < 2, parts)
        add_edges(below - 8, sub8 >= 6, parts)

    @pl.when(gx > 0)
    def _():
        cross_copy(1, 0).wait_recv()
        parts = [cross_r[1, :, j * 128 : j * 128 + 128] for j in range(cj + 1)]
        add_edges(base, sub8 < 2, parts)
        add_edges(base - 8, sub8 >= 6, parts)

    def swept(start, j, near):
        rows = pl.ds(start, step)
        total = load[j, rows, :]
        for n, x in enumerate(near[j]):
            total = total + coef[n, j, rows, :] * x
        return total

    for src, dst in ((mw.at[1], wbuf.at[0]), (wbuf.at[0], wbuf.at[1])):
        for i in range((rm + 16) // step):
            start = base - 8 + i * step
            _mid, near = around(src, start)
            for j in range(cj + 1):
                dst[j, pl.ds(start, step), :] = swept(start, j, near)

    for i in range(rm // step):
        start = base + i * step
        rows = pl.ds(start, step)
        tile_rows = pl.ds(i * step, step)
        _mid, near = around(wbuf.at[1], start)
        for j in range(cj):
            lanes = slice(j * 128, j * 128 + 128)
            x = swept(start, j, near)
            wbuf[0, j, rows, :] = x
            hi, lo = split(x - mw[1, j, rows, :])
            f_parts[tile_rows, lanes] = hi
            f_parts[pl.ds(rm + i * step, step), lanes] = lo

    results = [
        pltpu.make_async_copy(
            wbuf.at[0, j, pl.ds(base, rm), :],
            warp_out.at[:, pl.ds(j * 128, 128)],
            out_sem.at[j],
        )
        for j in range(cj)
    ]
    for copy in results:
        copy.start()

    tile_ids = iota((rm, jb), 0)
    for i in range(jpd // jb):
        blk = slice(i * jb, i * jb + jb)
        oh = oh_col[:, blk]
        got = jnp.dot(f_parts[...], oh, preferred_element_type=F32)
        got = got[:rm] + got[rm:]
        row = lax.shift_right_logical(cell_r[gy, :, blk], shift_c)
        inc_of[:, blk] = jnp.sum(
            jnp.where(tile_ids == row, got, 0.0), axis=0, keepdims=True
        )

    @pl.when(gx < last_x)
    def _():
        edge_copy(0, 0).wait_recv()

    @pl.when(gx > 0)
    def _():
        edge_copy(1, 0).wait_recv()

    def outer_row(row):
        return jnp.where(row < 2, row, jnp.where(row >= rm - 2, row - (rm - 8), -1))

    sub_c = iota((8, cm), 0)
    select(
        stacked(jnp.where(sub_c < 4, edge_r[1], edge_r[0])),
        outer_row,
        cell_r.at[gy],
        theta_of,
    )

    @pl.loop(1, n_gy)
    def _(d):
        reply_arrival(lax.rem(gy + d, n_gy)).wait_recv()

    theta = theta_of[...]
    for s in range(n_gy):
        theta = theta + reply_r[s]
    theta_of[...] = theta

    kk = iota((128, jb), 0)
    total = jnp.zeros((devices, 128), F32)
    for i in range(jpd // jb):
        blk = slice(i * jb, i * jb + jb)
        rank = slot_of[:, blk].astype(jnp.int32)
        value = jnp.where(kk < cap, inc_of[:, blk], theta_of[:, blk])
        here = (kk == rank) | (kk == rank + cap)
        value = jnp.where(here, value, (kk == 2 * cap).astype(F32))
        hi, lo = split(value)
        oh = oh_own[:, blk]
        for part in (hi, lo):
            total = total + lax.dot_general(
                oh, part, (((1,), (1,)), ((), ())), preferred_element_type=F32
            )
    for o in range(devices):
        out_s[o] = total[o : o + 1]

    me = gx * n_gy + gy

    def send_joints(to):
        o = to[0] * n_gy + to[1]
        remote(out_s.at[o], rows_out.at[me], joint_ss, joint_rs, to).start()

    for_others(send_joints)

    own = pltpu.make_async_copy(out_s.at[me], rows_out.at[me], aux_sem.at[2])
    own.start()

    for copy in results:
        copy.wait()

    @pl.when(gy > 0)
    def _():
        col_copy(0, gy - 1).wait_send()

    @pl.when(gy < last_y)
    def _():
        col_copy(1, gy + 1).wait_send()

    @pl.when(gx > 0)
    def _():
        row_copy(0, gx - 1).wait_send()

    @pl.when(gx < last_x)
    def _():
        row_copy(1, gx + 1).wait_send()

    @pl.loop(1, n_gy)
    def _(k):
        msg_copy(k).wait_send()
        ask_copy(k).wait_send()
        reply_copy(k).wait_send()

    for side, sends in ((0, sends_up), (1, sends_down)):

        @pl.when(sends)
        def _():
            @pl.loop(0, n_gy)
            def _(k):
                cross_copy(side, k).wait_send()
                edge_copy(side, k).wait_send()

    own.wait()
    every = pl.ds(0, devices - 1)
    all_joints = remote(
        out_s.at[every], rows_out.at[every], joint_ss, joint_rs, (gx, gy)
    )
    all_joints.wait_send()
    all_joints.wait_recv()


def finish_kernel(
    warp_hbm,
    rows_hbm,
    strain_hbm,
    resist_hbm,
    warp_out,
    strain_out,
    resist_out,
    rows_ref,
    strain_ref,
    resist_ref,
    held,
    sem,
):
    loads = [
        pltpu.make_async_copy(src, dst, sem.at[i])
        for i, (src, dst) in enumerate(
            (
                (rows_hbm, rows_ref),
                (strain_hbm, strain_ref),
                (resist_hbm, resist_ref),
            )
        )
    ]
    for load in loads:
        load.start()
    parts_of_warp = 4
    share = warp_hbm.shape[0] // parts_of_warp
    warp_rows = [pl.ds(n * share, share) for n in range(parts_of_warp)]
    into = [
        pltpu.make_async_copy(warp_hbm.at[r], held.at[r], sem.at[3 + n])
        for n, r in enumerate(warp_rows)
    ]
    out = [
        pltpu.make_async_copy(held.at[r], warp_out.at[r], sem.at[3 + n])
        for n, r in enumerate(warp_rows)
    ]
    for copy in into:
        copy.start()
    for first, then in zip(into, out):
        first.wait()
        then.start()
    for load in loads:
        load.wait()
    devices = rows_ref.shape[0]
    cap = resist_ref.shape[0] * 128 // devices
    groups = devices // 8
    per = 8 * cap // 128
    parts = [rows_ref[pl.ds(i, groups, stride=8), :] for i in range(8)]
    counts = [jnp.broadcast_to(p[:, 2 * cap : 2 * cap + 1], (groups, 128)) for p in parts]
    lane = iota((groups, 128), 1)
    for m in range(per):
        inc = theta = jnp.zeros((groups, 128), F32)
        live = jnp.zeros((groups, 128), F32)
        for i in range(8):
            lo, hi = max(i * cap, m * 128), min((i + 1) * cap, m * 128 + 128)
            if lo >= hi:
                continue
            here = (lane >= lo - m * 128) & (lane < hi - m * 128)
            shift = (i * cap - m * 128) % 128
            inc = jnp.where(here, pltpu.roll(parts[i], shift, 1), inc)
            theta = jnp.where(here, pltpu.roll(parts[i], (shift - cap) % 128, 1), theta)
            slot = (lane + (m * 128 - i * cap)).astype(F32)
            live = jnp.where(here, jnp.where(slot < counts[i], 1.0, 0.0), live)
        rows = pl.ds(m, groups, stride=per)
        total0, inelastic, resist = (
            strain_ref[0, rows, :],
            strain_ref[1, rows, :],
            resist_ref[rows, :],
        )
        total_new = total0 + inc
        arrhen = jnp.exp(2.0 - 2.0 / (1.0 + 0.1 * theta * theta))
        arg = shear_mod * (total_new - inelastic) / resist
        hyper = jnp.exp(arg - LN2) - jnp.exp(-arg - LN2)
        rate = rate_scale * arrhen * hyper * jnp.abs(hyper)
        size = jnp.abs(rate)
        target = sat_level * jnp.exp(sat_power * jnp.log(1.0 + size / arrhen))
        resist_new = resist + harden * (1.0 - resist / target) * size
        keep = live > 0.5
        strain_out[0, rows, :] = jnp.where(keep, total_new, total0)
        strain_out[1, rows, :] = jnp.where(keep, inelastic + rate, inelastic)
        resist_out[rows, :] = jnp.where(keep, resist_new, resist)
    for copy in out:
        copy.wait()


def solution(mesh):
    n_gx, n_gy = mesh.shape["gx"], mesh.shape["gy"]
    devices = n_gx * n_gy

    def body(
        temp_start,
        heat_input,
        lateral,
        vertical,
        weighting,
        modulus,
        warp_prev,
        joint_cell,
        joint_owner,
        joint_strain,
        joint_resist,
    ):
        layers, tr, columns = temp_start.shape
        rm, cm = modulus.shape
        jpd = joint_cell.shape[0]
        rows = joint_resist.shape[1] // 128
        blocks = tr // 8
        mwide = blocks * cm + cm // 2 + 128
        ext, cb, tall = cm + 128, cm // 128 + 1, rm + 32
        hbm = pl.BlockSpec(memory_space=pl.ANY)
        smem = pl.BlockSpec(memory_space=pltpu.SMEM)
        vmem = pl.BlockSpec(memory_space=pltpu.VMEM)
        dma = pltpu.SemaphoreType.DMA
        scratch = [
            pltpu.VMEM((n_gy, layers, tr, cm), F32),
            pltpu.VMEM((n_gy, layers, tr, cm), F32),
            pltpu.VMEM((2, 3, tr, columns + 256), F32),
            pltpu.VMEM((n_gy, 8, mwide), F32),
            pltpu.VMEM((n_gy, 8, mwide), F32),
            pltpu.VMEM((n_gy, 8, ext), F32),
            pltpu.VMEM((2, 8, ext), F32),
            pltpu.VMEM((n_gy, 8, cm), F32),
            pltpu.VMEM((2, 8, cm), F32),
            pltpu.VMEM((2, 2, 8, 128), F32),
            pltpu.VMEM((2, 2, 8, 128), F32),
            pltpu.VMEM((2, cb, tall, 128), F32),
            pltpu.VMEM((2, cb, tall, 128), F32),
            pltpu.VMEM((5, cb, tall, 128), F32),
            pltpu.VMEM((cb, tall, 128), F32),
            pltpu.VMEM((2 * rm, cm), BF16),
            pltpu.VMEM((cm, jpd), BF16),
            pltpu.VMEM((devices, jpd), BF16),
            pltpu.VMEM((1, jpd), F32),
            pltpu.VMEM((1, jpd), jnp.int32),
            pltpu.VMEM((n_gy, 1, jpd), jnp.int32),
            pltpu.VMEM((n_gy, 1, jpd), F32),
            pltpu.VMEM((n_gy, 1, jpd), F32),
            pltpu.VMEM((1, jpd), F32),
            pltpu.VMEM((1, jpd), F32),
            pltpu.VMEM((devices, 1, 128), F32),
            dma((2, n_gy)),
            dma((2, cb - 1)),
            dma((3,)),
            dma((cb - 1,)),
            dma((2,)),
            dma((2,)),
            dma((2,)),
            dma((2,)),
            dma((n_gy,)),
            dma((n_gy,)),
            dma((n_gy,)),
            dma((2,)),
            dma((n_gy,)),
            dma((2,)),
            dma((n_gy,)),
            dma((n_gy,)),
            dma((n_gy,)),
            dma((n_gy,)),
            dma,
            dma,
        ]
        warp, sent = pl.pallas_call(
            functools.partial(kernel, n_gx, n_gy, rows * 128 // devices),
            out_shape=(
                jax.ShapeDtypeStruct((rm, cm), F32),
                jax.ShapeDtypeStruct((devices, 1, 128), F32),
            ),
            in_specs=[hbm, hbm, smem, smem, smem, hbm, hbm, hbm, hbm],
            out_specs=(hbm, hbm),
            scratch_shapes=scratch,
            compiler_params=pltpu.CompilerParams(
                collective_id=0, has_side_effects=True, vmem_limit_bytes=56 * 2**20
            ),
        )(
            temp_start,
            heat_input,
            lateral,
            vertical,
            weighting,
            modulus,
            warp_prev,
            joint_cell.reshape(1, jpd),
            joint_owner.reshape(1, jpd),
        )
        warp, strain, resist = pl.pallas_call(
            finish_kernel,
            out_shape=(
                jax.ShapeDtypeStruct((rm, cm), F32),
                jax.ShapeDtypeStruct((2, rows, 128), F32),
                jax.ShapeDtypeStruct((rows, 128), F32),
            ),
            in_specs=[hbm, hbm, hbm, hbm],
            out_specs=(hbm, vmem, vmem),
            scratch_shapes=[
                pltpu.VMEM((devices, 128), F32),
                pltpu.VMEM((2, rows, 128), F32),
                pltpu.VMEM((rows, 128), F32),
                pltpu.VMEM((rm, cm), F32),
                dma((7,)),
            ],
            compiler_params=pltpu.CompilerParams(vmem_limit_bytes=60 * 2**20),
        )(
            warp,
            sent.reshape(devices, 128),
            joint_strain.reshape(2, rows, 128),
            joint_resist.reshape(rows, 128),
        )
        return (
            warp,
            strain.reshape(joint_strain.shape),
            resist.reshape(joint_resist.shape),
        )

    return jax.shard_map(
        body,
        mesh=mesh,
        in_specs=(
            P(None, ("gx", "gy"), None),
            P(None, ("gx", "gy"), None),
            P(),
            P(),
            P(),
            P("gx", "gy"),
            P("gx", "gy"),
            P(("gx", "gy")),
            P(("gx", "gy"), None),
            P(None, ("gx", "gy"), None),
            P(("gx", "gy"), None),
        ),
        out_specs=(P("gx", "gy"), P(None, ("gx", "gy"), None), P(("gx", "gy"), None)),
        check_vma=False,
    )
```

```python
import functools

import jax
import jax.numpy as jnp
from jax import lax
from jax.experimental import pallas as pl
from jax.experimental.pallas import tpu as pltpu
from jax.sharding import PartitionSpec as P

MESH = pl.DeviceIdType.MESH
F32 = jnp.float32
BF16 = jnp.bfloat16

stiffness = 0.2
shear_mod = 0.6
rate_scale = 0.5
sat_level = 2.5
sat_power = 0.3
harden = 2.0
LN2 = 0.6931471805599453


def iota(shape, dim):
    return lax.broadcasted_iota(jnp.int32, shape, dim)


def split(x):
    hi = x.astype(BF16)
    return hi, (x - hi.astype(F32)).astype(BF16)


def layer_weights(lat, ver, w):
    n = len(w)

    def add(x, y):
        return y if x is None else x if y is None else x + y

    def mul(x, y):
        return None if x is None else x * y

    def vert(x):
        out = []
        for l in range(n):
            keep = 1.0
            if l < n - 1:
                keep = keep - ver[l]
            if l > 0:
                keep = keep - ver[l - 1]
            total = mul(x[l], keep)
            if l > 0:
                total = add(total, mul(x[l - 1], ver[l - 1]))
            if l < n - 1:
                total = add(total, mul(x[l + 1], ver[l]))
            out.append(total)
        return out

    u = vert(w)
    wd = [mul(x, d) for x, d in zip(w, lat)]
    a0 = vert(u)
    a1 = [add(mul(x, d), y) for x, d, y in zip(u, lat, vert(wd))]
    a2 = [mul(x, d) for x, d in zip(wd, lat)]
    b0 = [add(x, y) for x, y in zip(u, w)]
    return (a0, b0), (a1, wd), (a2, [None] * n)


def kernel(
    n_gx,
    n_gy,
    cap,
    temp_ref,
    heat_ref,
    lat_ref,
    ver_ref,
    wei_ref,
    mod_ref,
    prev_ref,
    cell_ref,
    owner_ref,
    warp_out,
    rows_out,
    tbuf,
    hbuf,
    sums,
    msg_s,
    msg_r,
    cross_s,
    cross_r,
    edge_s,
    edge_r,
    col_s,
    col_r,
    mw,
    wbuf,
    coef,
    load,
    f_parts,
    oh_col,
    oh_own,
    slot_of,
    owner_of,
    cell_r,
    reply_s,
    reply_r,
    inc_of,
    theta_of,
    out_s,
    load_sem,
    mw_sem,
    aux_sem,
    out_sem,
    col_ss,
    col_rs,
    row_ss,
    row_rs,
    msg_ss,
    msg_rs,
    cross_ss,
    cross_rs,
    edge_ss,
    edge_rs,
    ask_ss,
    ask_rs,
    reply_ss,
    reply_rs,
    joint_ss,
    joint_rs,
):
    layers, tr, columns = temp_ref.shape
    rm, cm = mod_ref.shape
    blocks = tr // 8
    ext = cm + 128
    cj = cm // 128
    devices = n_gx * n_gy
    jpd = cell_ref.shape[1]
    gx, gy = lax.axis_index("gx"), lax.axis_index("gy")
    last_x, last_y = n_gx - 1, n_gy - 1
    base = 16
    below = base + rm

    def remote(src, dst, ss, rs, to):
        return pltpu.make_async_remote_copy(
            src_ref=src,
            dst_ref=dst,
            send_sem=ss,
            recv_sem=rs,
            device_id=to,
            device_id_type=MESH,
        )

    def chunk_of(k):
        return lax.rem(gy + k, n_gy)

    def chunk_copies(k):
        cols = pl.ds(pl.multiple_of(chunk_of(k) * cm, cm), cm)
        return (
            pltpu.make_async_copy(temp_ref.at[:, :, cols], tbuf.at[k], load_sem.at[0, k]),
            pltpu.make_async_copy(heat_ref.at[:, :, cols], hbuf.at[k], load_sem.at[1, k]),
        )

    def mw_copies():
        return [
            pltpu.make_async_copy(
                ref.at[:, pl.ds(j * 128, 128)],
                mw.at[i, j, pl.ds(base, rm), :],
                mw_sem.at[i, j],
            )
            for i, ref in enumerate((mod_ref, prev_ref))
            for j in range(cj)
        ]

    aux = (
        pltpu.make_async_copy(cell_ref, cell_r.at[gy], aux_sem.at[0]),
        pltpu.make_async_copy(owner_ref, owner_of, aux_sem.at[1]),
    )

    @pl.loop(0, 3)
    def _(k):
        for copy in chunk_copies(k):
            copy.start()

    for copy in mw_copies():
        copy.start()
    for copy in aux:
        copy.start()

    @pl.loop(3, n_gy)
    def _(k):
        for copy in chunk_copies(k):
            copy.start()

    @pl.when(gy == last_y)
    def _():
        col_r[0] = jnp.zeros_like(col_r[0])

    @pl.when(gy == 0)
    def _():
        col_r[1] = jnp.zeros_like(col_r[1])

    zero8 = jnp.zeros((8, 128), F32)

    @pl.when(gx == last_x)
    def _():
        for i in range(2):
            for j in range(cj + 1):
                mw[i, j, below : below + 8, :] = zero8
        cross_r[0] = jnp.zeros_like(cross_r[0])
        edge_r[0] = jnp.zeros_like(edge_r[0])

    @pl.when(gx == 0)
    def _():
        for i in range(2):
            for j in range(cj + 1):
                mw[i, j, base - 8 : base, :] = zero8
        cross_r[1] = jnp.zeros_like(cross_r[1])
        edge_r[1] = jnp.zeros_like(edge_r[1])

    barrier = pltpu.get_barrier_semaphore()

    def wrapped(i, n):
        return jnp.where(i >= n, i - n, i)

    def for_others(act):
        for dy in range(1, n_gy):
            act((gx, wrapped(gy + dy, n_gy)))

        @pl.loop(1, n_gx)
        def _(dx):
            x = wrapped(gx + dx, n_gx)
            for dy in range(n_gy):
                act((x, wrapped(gy + dy, n_gy)))

    def greet(to):
        pl.semaphore_signal(barrier, inc=1, device_id=to, device_id_type=MESH)

    for_others(greet)

    lat = [lat_ref[i] for i in range(layers)]
    ver = [ver_ref[i] for i in range(layers - 1)]
    wei = [wei_ref[i] for i in range(layers)]
    fields = [
        layer_weights(lat, ver, wei),
        layer_weights(lat, ver, [None] * (layers - 1) + [1.0]),
    ]

    zero_cols = jnp.zeros((tr, 128), F32)
    for f in range(2):
        for p in range(3):
            sums[f, p, :, 0:128] = zero_cols
            sums[f, p, :, columns + 128 : columns + 256] = zero_cols
    for j in range(cj + 1):
        for rows in (slice(0, 8), slice(below + 8, below + 16)):
            for ref in (mw.at[0], mw.at[1], wbuf.at[0], wbuf.at[1]):
                ref[j, rows, :] = zero8

    def await_chunk(k):
        for copy in chunk_copies(k):
            copy.wait()

    def layer_sums(k):
        start = 128 + chunk_of(k) * cm
        for j in range(cj):
            lanes = slice(j * 128, j * 128 + 128)
            acc = [[None] * 3, [None] * 3]
            for l in range(layers):
                t, h = tbuf[k, l, :, lanes], hbuf[k, l, :, lanes]
                for f in range(2):
                    for p in range(3):
                        a, b = fields[f][p]
                        for c, x in ((a[l], t), (b[l], h)):
                            if c is not None:
                                term = c * x
                                acc[f][p] = (
                                    term if acc[f][p] is None else acc[f][p] + term
                                )
            where = pl.ds(pl.multiple_of(start + j * 128, 128), 128)
            for f in range(2):
                for p in range(3):
                    sums[f, p, :, where] = acc[f][p]

    wide = cm + 256
    crow = tr + 8

    def neighbours(x):
        r, c = x.shape
        return (
            pltpu.roll(x, 1, 0)
            + pltpu.roll(x, r - 1, 0)
            + pltpu.roll(x, 1, 1)
            + pltpu.roll(x, c - 1, 1)
            - 4.0 * x
        )

    def contribution(f, c):
        window = pl.ds(pl.multiple_of(c * cm, cm), wide)
        zero = jnp.zeros((8, wide), F32)
        p0, p1, p2 = (
            jnp.concatenate([sums[f, p, :, window], zero], axis=0) for p in range(3)
        )
        q = p1 + neighbours(p2)
        col = c * cm - 128 + iota((crow, wide), 1)
        row = iota((crow, wide), 0)
        panel = (col >= 0) & (col < columns)
        panel = panel & ((row < tr + 4) | (gx > 0) | (gy > 0))
        panel = panel & (
            (row < tr) | (row >= tr + 4) | (gx < last_x) | (gy < last_y)
        )
        q = jnp.where(panel, q, 0.0)
        out = p0 + neighbours(q)
        main = out[:, 128 : 128 + cm]
        lane = iota((crow, 128), 1)
        halo = jnp.where(lane < 64, out[:, 128 + cm :], out[:, 0:128])
        return main, halo

    lane8 = iota((8, 128), 1)
    sub8 = iota((8, 128), 0)
    sub_h = iota((8, cm // 2), 0)
    sub_e = iota((8, ext), 0)
    half = cm // 2
    at = blocks * cm

    def write_message(ref, main, halo):
        for b in range(blocks):
            ref[:, b * cm : b * cm + cm] = main[8 * b : 8 * b + 8]
        edge = main[tr:]
        ref[:, at : at + half] = jnp.where(
            (sub_h < 2) | (sub_h >= 6), edge[:, :half], pltpu.roll(edge[:, half:], 4, 0)
        )
        packed = halo[0:8]
        for b in range(1, blocks + 1):
            here = (lane8 >= 8 * b - 2) & (lane8 < 8 * b + 2)
            packed = jnp.where(
                here, pltpu.roll(halo[8 * b : 8 * b + 8], 8 * b, 1), packed
            )
        ref[:, at + half : at + half + 128] = packed

    def msg_copy(k):
        return remote(
            msg_s.at[k], msg_r.at[gy], msg_ss.at[k], msg_rs.at[gy], (gx, chunk_of(k))
        )

    def msg_arrival(s):
        return remote(msg_s.at[0], msg_r.at[s], msg_ss.at[0], msg_rs.at[s], (gx, s))

    def beyond(side):
        return gx - 1 if side == 0 else gx + 1

    def cross_copy(side, k):
        return remote(
            cross_s.at[k],
            cross_r.at[side],
            cross_ss.at[k],
            cross_rs.at[side],
            (beyond(side), chunk_of(k)),
        )

    def edge_copy(side, k):
        return remote(
            edge_s.at[k],
            edge_r.at[side],
            edge_ss.at[k],
            edge_rs.at[side],
            (beyond(side), chunk_of(k)),
        )

    sends_up = (gy == 0) & (gx > 0)
    sends_down = (gy == last_y) & (gx < last_x)

    def prepare(k, to_ref):
        main, halo = contribution(0, chunk_of(k))
        write_message(to_ref, main, halo)

        block = jnp.concatenate([main, halo], axis=1)
        inner = jnp.where(gy == 0, block[0:8], block[tr - 8 : tr])
        cross_s[k] = jnp.where((sub_e < 4) == (gy == 0), inner, block[tr:])

    def send_cross(copy_of, k):
        @pl.when(sends_up)
        def _():
            copy_of(0, k).start()

        @pl.when(sends_down)
        def _():
            copy_of(1, k).start()

    for k in range(3):
        await_chunk(k)
        layer_sums(k)
    prepare(1, msg_s.at[1])

    pl.semaphore_wait(barrier, devices - 1)

    msg_copy(1).start()
    send_cross(cross_copy, 1)

    def ask_copy(d):
        return remote(
            cell_ref, cell_r.at[gy], ask_ss.at[d], ask_rs.at[gy], (gx, chunk_of(d))
        )

    def ask_arrival(s):
        return remote(cell_ref, cell_r.at[s], ask_ss.at[0], ask_rs.at[s], (gx, s))

    for copy in mw_copies():
        copy.wait()
    for i in range(2):
        to_left, to_right = zero8, zero8
        for b in range(rm // 8):
            here = (lane8 >= 4 * b) & (lane8 < 4 * b + 4)
            rows = slice(base + 8 * b, base + 8 * b + 8)
            to_left = jnp.where(here, pltpu.roll(mw[i, 0, rows, :], 4 * b, 1), to_left)
            to_right = jnp.where(
                here,
                pltpu.roll(mw[i, cj - 1, rows, :], (4 * b + 4) % 128, 1),
                to_right,
            )
        col_s[0, i] = to_left
        col_s[1, i] = to_right

    def col_copy(side, to):
        return remote(
            col_s.at[side], col_r.at[side], col_ss.at[side], col_rs.at[side], (gx, to)
        )

    @pl.when(gy > 0)
    def _():
        col_copy(0, gy - 1).start()

    @pl.when(gy < last_y)
    def _():
        col_copy(1, gy + 1).start()

    @pl.loop(1, n_gy)
    def _(d):
        ask_copy(d).start()

    def send_load(k):
        msg_copy(k).start()
        send_cross(cross_copy, k)

    pairs = (n_gy - 4) // 2

    @pl.loop(0, pairs)
    def _(i):
        ks = (2 * i + 3, 2 * i + 4)
        for k in ks:
            await_chunk(k)
        for k in ks:
            layer_sums(k)
            prepare(k - 1, msg_s.at[k - 1])
        for k in ks:
            send_load(k - 1)

    for k in range(2 * pairs + 3, n_gy):
        await_chunk(k)
        layer_sums(k)
        prepare(k - 1, msg_s.at[k - 1])
        send_load(k - 1)
    prepare(n_gy - 1, msg_s.at[n_gy - 1])
    send_load(n_gy - 1)
    prepare(0, msg_r.at[gy])
    send_cross(cross_copy, 0)

    @pl.when(gy < last_y)
    def _():
        col_copy(0, gy).wait_recv()

    @pl.when(gy > 0)
    def _():
        col_copy(1, gy).wait_recv()

    for i in range(2):
        right, left = col_r[0, i], col_r[1, i]
        for b in range(rm // 8):
            mw[i, cj, base + 8 * b : base + 8 * b + 8, :] = jnp.where(
                lane8 < 64,
                pltpu.roll(right, (128 - 4 * b) % 128, 1),
                pltpu.roll(left, (256 - 4 * b - 4) % 128, 1),
            )

    def row_copy(side, to):
        src = base if side == 0 else below - 8
        dst = below if side == 0 else base - 8
        return remote(
            mw.at[:, :, pl.ds(src, 8), :],
            mw.at[:, :, pl.ds(dst, 8), :],
            row_ss.at[side],
            row_rs.at[side],
            (to, gy),
        )

    @pl.when(gx > 0)
    def _():
        row_copy(0, gx - 1).start()

    @pl.when(gx < last_x)
    def _():
        row_copy(1, gx + 1).start()

    for copy in aux:
        copy.wait()

    @pl.loop(1, n_gy)
    def _(d):
        ask_arrival(lax.rem(gy + d, n_gy)).wait_recv()

    jb = 256
    shift_c = cm.bit_length() - 1
    lane_rows = iota((128, jb), 0)

    def one_hot(rows, at_row):
        return (rows == at_row).astype(F32).astype(BF16)

    def select(table, row_of, cells_ref, to_ref):
        tall = table.shape[0]
        per = tall // cj
        lhs = jnp.concatenate(split(table), axis=1)
        ids = iota((tall, jb), 0)
        for i in range(jpd // jb):
            blk = slice(i * jb, i * jb + jb)
            cells = cells_ref[:, blk]
            row = row_of(lax.shift_right_logical(cells, shift_c))
            block = lax.shift_right_logical(cells & (cm - 1), 7)
            place = jnp.where(row >= 0, block * per + row, -1)
            oh = one_hot(lane_rows, cells & 127)
            got = jnp.dot(
                lhs, jnp.concatenate([oh, oh], axis=0), preferred_element_type=F32
            )
            to_ref[:, blk] = jnp.sum(
                jnp.where(ids == place, got, 0.0), axis=0, keepdims=True
            )

    def stacked(x):
        return jnp.concatenate([x[:, j * 128 : j * 128 + 128] for j in range(cj)], axis=0)

    def near_row(row):
        q = row - gy * tr
        inside = (q >= 0) & (q < tr + 2)
        before = (q < 0) & (q >= -2)
        return jnp.where(inside, q, jnp.where(before, q + crow, -1))

    def reply_copy(k):
        return remote(
            reply_s.at[k],
            reply_r.at[gy],
            reply_ss.at[k],
            reply_rs.at[gy],
            (gx, chunk_of(k)),
        )

    def reply_arrival(s):
        return remote(
            reply_s.at[0], reply_r.at[s], reply_ss.at[0], reply_rs.at[s], (gx, s)
        )

    group = 4

    @pl.loop(0, n_gy // group)
    def _(i):
        ks = [lax.rem(group * i + u + 1, n_gy) for u in range(group)]
        for k in ks:
            main, _halo = contribution(1, chunk_of(k))
            edge_s[k] = main[tr:]
            select(stacked(main), near_row, cell_r.at[chunk_of(k)], reply_s.at[k])
        for k in ks:
            send_cross(edge_copy, k)

            @pl.when(k > 0)
            def _():
                reply_copy(k).start()

    reply_r[gy] = reply_s[0]

    step = 16
    lane_s = iota((step, 128), 1)

    def around(ref, start):
        rows = pl.ds(start, step)
        mid = [ref[j, rows, :] for j in range(cj + 1)]
        up = [ref[j, pl.ds(start - 1, step), :] for j in range(cj + 1)]
        down = [ref[j, pl.ds(start + 1, step), :] for j in range(cj + 1)]
        to_r = [pltpu.roll(x, 1, 1) for x in mid]
        to_l = [pltpu.roll(x, 127, 1) for x in mid]
        left = [jnp.where(lane_s == 0, to_r[j - 1], to_r[j]) for j in range(cj + 1)]
        right = [
            jnp.where(lane_s == 127, to_l[(j + 1) % (cj + 1)], to_l[j])
            for j in range(cj + 1)
        ]
        return mid, list(zip(up, down, left, right))

    @pl.when(gx < last_x)
    def _():
        row_copy(0, gx).wait_recv()

    @pl.when(gx > 0)
    def _():
        row_copy(1, gx).wait_recv()

    halo_ok = ((lane_s < 64) & (gy < last_y)) | ((lane_s >= 64) & (gy > 0))

    for i in range((rm + 16) // step):
        start = base - 8 + i * step
        rows = pl.ds(start, step)
        mid, near = around(mw.at[0], start)
        row = start + iota((step, 128), 0)
        ok = ((row >= base) | (gx > 0)) & ((row < below) | (gx < last_x))
        for j in range(cj + 1):
            faces = [0.5 * (mid[j] + x) for x in near[j]]
            denom = stiffness + faces[0] + faces[1] + faces[2] + faces[3]
            inv = jnp.where(ok & halo_ok if j == cj else ok, 1.0 / denom, 0.0)
            for n, face in enumerate(faces):
                coef[n, j, rows, :] = face * inv
            coef[4, j, rows, :] = inv

    upper = (iota((jb, jb), 0) < iota((jb, jb), 1)).astype(F32).astype(BF16)
    own_rows = iota((devices, jb), 0)
    col_rows = iota((cm, jb), 0)
    carry = jnp.zeros((devices, 1), F32)
    for i in range(jpd // jb):
        blk = slice(i * jb, i * jb + jb)
        oh_col[:, blk] = one_hot(col_rows, cell_r[gy, :, blk] & (cm - 1))
        owner = owner_of[:, blk]
        oh = (own_rows == owner).astype(F32)
        oh_own[:, blk] = oh.astype(BF16)
        before = jnp.dot(oh.astype(BF16), upper, preferred_element_type=F32)
        slot_of[:, blk] = jnp.sum(oh * (before + carry), axis=0, keepdims=True)
        carry = carry + jnp.sum(oh, axis=1, keepdims=True)

    for j in range(cj + 1):
        for rows in (slice(base - 8, base), slice(below, below + 8)):
            load[j, rows, :] = zero8

    def assemble(s):
        packed = msg_r[s, :, at + half : at + half + 128]
        for b in range(blocks):
            rows = pl.ds(pl.multiple_of(base + s * tr + 8 * b, 8), 8)
            for j in range(cj):
                lanes = slice(b * cm + j * 128, b * cm + j * 128 + 128)
                load[j, rows, :] = msg_r[s, :, lanes] * coef[4, j, rows, :]
            halo = packed if b == 0 else pltpu.roll(packed, 128 - 8 * b, 1)
            load[cj, rows, :] = halo * coef[4, cj, rows, :]

    for start in range(0, n_gy, group):
        sources = [lax.rem(gy + n_gy - start - u, n_gy) for u in range(group)]
        for u, s in enumerate(sources):
            if start + u > 0:
                msg_arrival(s).wait_recv()
        for s in sources:
            assemble(s)

    def add_edges(start, keep, parts):
        rows = pl.ds(start, 8)
        for j, x in enumerate(parts):
            load[j, rows, :] = load[j, rows, :] + jnp.where(
                keep, x * coef[4, j, rows, :], 0.0
            )

    for s in range(n_gy):
        both = [msg_r[s, :, at + j * 128 : at + j * 128 + 128] for j in range(cj // 2)]
        parts = both + [pltpu.roll(x, 4, 0) for x in both]
        parts.append(
            pltpu.roll(msg_r[s, :, at + half : at + half + 128], 128 - 8 * blocks, 1)
        )
        add_edges(base + (s + 1) * tr, sub8 < 2, parts)
        add_edges(base + s * tr - 8, sub8 >= 6, parts)

    @pl.when(gx < last_x)
    def _():
        cross_copy(0, 0).wait_recv()
        parts = [cross_r[0, :, j * 128 : j * 128 + 128] for j in range(cj + 1)]
        add_edges(below, sub8 < 2, parts)
        add_edges(below - 8, sub8 >= 6, parts)

    @pl.when(gx > 0)
    def _():
        cross_copy(1, 0).wait_recv()
        parts = [cross_r[1, :, j * 128 : j * 128 + 128] for j in range(cj + 1)]
        add_edges(base, sub8 < 2, parts)
        add_edges(base - 8, sub8 >= 6, parts)

    def swept(start, j, near):
        rows = pl.ds(start, step)
        total = load[j, rows, :]
        for n, x in enumerate(near[j]):
            total = total + coef[n, j, rows, :] * x
        return total

    for src, dst in ((mw.at[1], wbuf.at[0]), (wbuf.at[0], wbuf.at[1])):
        for i in range((rm + 16) // step):
            start = base - 8 + i * step
            _mid, near = around(src, start)
            for j in range(cj + 1):
                dst[j, pl.ds(start, step), :] = swept(start, j, near)

    for i in range(rm // step):
        start = base + i * step
        rows = pl.ds(start, step)
        tile_rows = pl.ds(i * step, step)
        _mid, near = around(wbuf.at[1], start)
        for j in range(cj):
            lanes = slice(j * 128, j * 128 + 128)
            x = swept(start, j, near)
            wbuf[0, j, rows, :] = x
            hi, lo = split(x - mw[1, j, rows, :])
            f_parts[tile_rows, lanes] = hi
            f_parts[pl.ds(rm + i * step, step), lanes] = lo

    results = [
        pltpu.make_async_copy(
            wbuf.at[0, j, pl.ds(base, rm), :],
            warp_out.at[:, pl.ds(j * 128, 128)],
            out_sem.at[j],
        )
        for j in range(cj)
    ]
    for copy in results:
        copy.start()

    tile_ids = iota((rm, jb), 0)
    for i in range(jpd // jb):
        blk = slice(i * jb, i * jb + jb)
        oh = oh_col[:, blk]
        got = jnp.dot(f_parts[...], oh, preferred_element_type=F32)
        got = got[:rm] + got[rm:]
        row = lax.shift_right_logical(cell_r[gy, :, blk], shift_c)
        inc_of[:, blk] = jnp.sum(
            jnp.where(tile_ids == row, got, 0.0), axis=0, keepdims=True
        )

    @pl.when(gx < last_x)
    def _():
        edge_copy(0, 0).wait_recv()

    @pl.when(gx > 0)
    def _():
        edge_copy(1, 0).wait_recv()

    def outer_row(row):
        return jnp.where(row < 2, row, jnp.where(row >= rm - 2, row - (rm - 8), -1))

    sub_c = iota((8, cm), 0)
    select(
        stacked(jnp.where(sub_c < 4, edge_r[1], edge_r[0])),
        outer_row,
        cell_r.at[gy],
        theta_of,
    )

    @pl.loop(1, n_gy)
    def _(d):
        reply_arrival(lax.rem(gy + d, n_gy)).wait_recv()

    theta = theta_of[...]
    for s in range(n_gy):
        theta = theta + reply_r[s]
    theta_of[...] = theta

    kk = iota((128, jb), 0)
    total = jnp.zeros((devices, 128), F32)
    for i in range(jpd // jb):
        blk = slice(i * jb, i * jb + jb)
        rank = slot_of[:, blk].astype(jnp.int32)
        value = jnp.where(kk < cap, inc_of[:, blk], theta_of[:, blk])
        here = (kk == rank) | (kk == rank + cap)
        value = jnp.where(here, value, (kk == 2 * cap).astype(F32))
        hi, lo = split(value)
        oh = oh_own[:, blk]
        for part in (hi, lo):
            total = total + lax.dot_general(
                oh, part, (((1,), (1,)), ((), ())), preferred_element_type=F32
            )
    for o in range(devices):
        out_s[o] = total[o : o + 1]

    me = gx * n_gy + gy

    def send_joints(to):
        o = to[0] * n_gy + to[1]
        remote(out_s.at[o], rows_out.at[me], joint_ss, joint_rs, to).start()

    for_others(send_joints)

    own = pltpu.make_async_copy(out_s.at[me], rows_out.at[me], aux_sem.at[2])
    own.start()

    for copy in results:
        copy.wait()

    @pl.when(gy > 0)
    def _():
        col_copy(0, gy - 1).wait_send()

    @pl.when(gy < last_y)
    def _():
        col_copy(1, gy + 1).wait_send()

    @pl.when(gx > 0)
    def _():
        row_copy(0, gx - 1).wait_send()

    @pl.when(gx < last_x)
    def _():
        row_copy(1, gx + 1).wait_send()

    @pl.loop(1, n_gy)
    def _(k):
        msg_copy(k).wait_send()
        ask_copy(k).wait_send()
        reply_copy(k).wait_send()

    for side, sends in ((0, sends_up), (1, sends_down)):

        @pl.when(sends)
        def _():
            @pl.loop(0, n_gy)
            def _(k):
                cross_copy(side, k).wait_send()
                edge_copy(side, k).wait_send()

    own.wait()
    every = pl.ds(0, devices - 1)
    all_joints = remote(
        out_s.at[every], rows_out.at[every], joint_ss, joint_rs, (gx, gy)
    )
    all_joints.wait_send()
    all_joints.wait_recv()


def finish_kernel(
    warp_hbm,
    rows_hbm,
    strain_hbm,
    resist_hbm,
    warp_out,
    strain_out,
    resist_out,
    rows_ref,
    strain_ref,
    resist_ref,
    held,
    strain_new,
    resist_new_ref,
    sem,
):
    loads = [
        pltpu.make_async_copy(src, dst, sem.at[i])
        for i, (src, dst) in enumerate(
            (
                (rows_hbm, rows_ref),
                (strain_hbm, strain_ref),
                (resist_hbm, resist_ref),
            )
        )
    ]
    for load in loads:
        load.start()
    parts_of_warp = 4
    share = warp_hbm.shape[0] // parts_of_warp
    warp_rows = [pl.ds(n * share, share) for n in range(parts_of_warp)]
    into = [
        pltpu.make_async_copy(warp_hbm.at[r], held.at[r], sem.at[3 + n])
        for n, r in enumerate(warp_rows)
    ]
    out = [
        pltpu.make_async_copy(held.at[r], warp_out.at[r], sem.at[3 + n])
        for n, r in enumerate(warp_rows)
    ]
    for copy in into:
        copy.start()
    for first, then in zip(into, out):
        first.wait()
        then.start()
    for load in loads:
        load.wait()
    devices = rows_ref.shape[0]
    cap = resist_ref.shape[0] * 128 // devices
    groups = devices // 8
    per = 8 * cap // 128
    parts = [rows_ref[pl.ds(i, groups, stride=8), :] for i in range(8)]
    counts = [jnp.broadcast_to(p[:, 2 * cap : 2 * cap + 1], (groups, 128)) for p in parts]
    lane = iota((groups, 128), 1)
    for m in range(per):
        inc = theta = jnp.zeros((groups, 128), F32)
        live = jnp.zeros((groups, 128), F32)
        for i in range(8):
            lo, hi = max(i * cap, m * 128), min((i + 1) * cap, m * 128 + 128)
            if lo >= hi:
                continue
            here = (lane >= lo - m * 128) & (lane < hi - m * 128)
            shift = (i * cap - m * 128) % 128
            inc = jnp.where(here, pltpu.roll(parts[i], shift, 1), inc)
            theta = jnp.where(here, pltpu.roll(parts[i], (shift - cap) % 128, 1), theta)
            slot = (lane + (m * 128 - i * cap)).astype(F32)
            live = jnp.where(here, jnp.where(slot < counts[i], 1.0, 0.0), live)
        rows = pl.ds(m, groups, stride=per)
        total0, inelastic, resist = (
            strain_ref[0, rows, :],
            strain_ref[1, rows, :],
            resist_ref[rows, :],
        )
        total_new = total0 + inc
        arrhen = jnp.exp(2.0 - 2.0 / (1.0 + 0.1 * theta * theta))
        arg = shear_mod * (total_new - inelastic) / resist
        hyper = jnp.exp(arg - LN2) - jnp.exp(-arg - LN2)
        rate = rate_scale * arrhen * hyper * jnp.abs(hyper)
        size = jnp.abs(rate)
        target = sat_level * jnp.exp(sat_power * jnp.log(1.0 + size / arrhen))
        resist_new = resist + harden * (1.0 - resist / target) * size
        keep = live > 0.5
        strain_new[0, rows, :] = jnp.where(keep, total_new, total0)
        strain_new[1, rows, :] = jnp.where(keep, inelastic + rate, inelastic)
        resist_new_ref[rows, :] = jnp.where(keep, resist_new, resist)
    small = [
        pltpu.make_async_copy(strain_new, strain_out, sem.at[1]),
        pltpu.make_async_copy(resist_new_ref, resist_out, sem.at[2]),
    ]
    for copy in small:
        copy.start()
    for copy in out + small:
        copy.wait()


def solution(mesh):
    n_gx, n_gy = mesh.shape["gx"], mesh.shape["gy"]
    devices = n_gx * n_gy

    def body(
        temp_start,
        heat_input,
        lateral,
        vertical,
        weighting,
        modulus,
        warp_prev,
        joint_cell,
        joint_owner,
        joint_strain,
        joint_resist,
    ):
        layers, tr, columns = temp_start.shape
        rm, cm = modulus.shape
        jpd = joint_cell.shape[0]
        rows = joint_resist.shape[1] // 128
        blocks = tr // 8
        mwide = blocks * cm + cm // 2 + 128
        ext, cb, tall = cm + 128, cm // 128 + 1, rm + 32
        hbm = pl.BlockSpec(memory_space=pl.ANY)
        smem = pl.BlockSpec(memory_space=pltpu.SMEM)
        dma = pltpu.SemaphoreType.DMA
        scratch = [
            pltpu.VMEM((n_gy, layers, tr, cm), F32),
            pltpu.VMEM((n_gy, layers, tr, cm), F32),
            pltpu.VMEM((2, 3, tr, columns + 256), F32),
            pltpu.VMEM((n_gy, 8, mwide), F32),
            pltpu.VMEM((n_gy, 8, mwide), F32),
            pltpu.VMEM((n_gy, 8, ext), F32),
            pltpu.VMEM((2, 8, ext), F32),
            pltpu.VMEM((n_gy, 8, cm), F32),
            pltpu.VMEM((2, 8, cm), F32),
            pltpu.VMEM((2, 2, 8, 128), F32),
            pltpu.VMEM((2, 2, 8, 128), F32),
            pltpu.VMEM((2, cb, tall, 128), F32),
            pltpu.VMEM((2, cb, tall, 128), F32),
            pltpu.VMEM((5, cb, tall, 128), F32),
            pltpu.VMEM((cb, tall, 128), F32),
            pltpu.VMEM((2 * rm, cm), BF16),
            pltpu.VMEM((cm, jpd), BF16),
            pltpu.VMEM((devices, jpd), BF16),
            pltpu.VMEM((1, jpd), F32),
            pltpu.VMEM((1, jpd), jnp.int32),
            pltpu.VMEM((n_gy, 1, jpd), jnp.int32),
            pltpu.VMEM((n_gy, 1, jpd), F32),
            pltpu.VMEM((n_gy, 1, jpd), F32),
            pltpu.VMEM((1, jpd), F32),
            pltpu.VMEM((1, jpd), F32),
            pltpu.VMEM((devices, 1, 128), F32),
            dma((2, n_gy)),
            dma((2, cb - 1)),
            dma((3,)),
            dma((cb - 1,)),
            dma((2,)),
            dma((2,)),
            dma((2,)),
            dma((2,)),
            dma((n_gy,)),
            dma((n_gy,)),
            dma((n_gy,)),
            dma((2,)),
            dma((n_gy,)),
            dma((2,)),
            dma((n_gy,)),
            dma((n_gy,)),
            dma((n_gy,)),
            dma((n_gy,)),
            dma,
            dma,
        ]
        warp, sent = pl.pallas_call(
            functools.partial(kernel, n_gx, n_gy, rows * 128 // devices),
            out_shape=(
                jax.ShapeDtypeStruct((rm, cm), F32),
                jax.ShapeDtypeStruct((devices, 1, 128), F32),
            ),
            in_specs=[hbm, hbm, smem, smem, smem, hbm, hbm, hbm, hbm],
            out_specs=(hbm, hbm),
            scratch_shapes=scratch,
            compiler_params=pltpu.CompilerParams(
                collective_id=0, has_side_effects=True, vmem_limit_bytes=56 * 2**20
            ),
        )(
            temp_start,
            heat_input,
            lateral,
            vertical,
            weighting,
            modulus,
            warp_prev,
            joint_cell.reshape(1, jpd),
            joint_owner.reshape(1, jpd),
        )
        warp, strain, resist = pl.pallas_call(
            finish_kernel,
            out_shape=(
                jax.ShapeDtypeStruct((rm, cm), F32),
                jax.ShapeDtypeStruct((2, rows, 128), F32),
                jax.ShapeDtypeStruct((rows, 128), F32),
            ),
            in_specs=[hbm, hbm, hbm, hbm],
            out_specs=(hbm, hbm, hbm),
            scratch_shapes=[
                pltpu.VMEM((devices, 128), F32),
                pltpu.VMEM((2, rows, 128), F32),
                pltpu.VMEM((rows, 128), F32),
                pltpu.VMEM((rm, cm), F32),
                pltpu.VMEM((2, rows, 128), F32),
                pltpu.VMEM((rows, 128), F32),
                dma((7,)),
            ],
            compiler_params=pltpu.CompilerParams(vmem_limit_bytes=60 * 2**20),
        )(
            warp,
            sent.reshape(devices, 128),
            joint_strain.reshape(2, rows, 128),
            joint_resist.reshape(rows, 128),
        )
        return (
            warp,
            strain.reshape(joint_strain.shape),
            resist.reshape(joint_resist.shape),
        )

    return jax.shard_map(
        body,
        mesh=mesh,
        in_specs=(
            P(None, ("gx", "gy"), None),
            P(None, ("gx", "gy"), None),
            P(),
            P(),
            P(),
            P("gx", "gy"),
            P("gx", "gy"),
            P(("gx", "gy")),
            P(("gx", "gy"), None),
            P(None, ("gx", "gy"), None),
            P(("gx", "gy"), None),
        ),
        out_specs=(P("gx", "gy"), P(None, ("gx", "gy"), None), P(("gx", "gy"), None)),
        check_vma=False,
    )
```
